512 devices in a mesh: blk: 8 (over y, x_lo), rep: 64 (over z, x_hi, core).
Axes of the slice: x: 4 (x_hi: 2, x_lo: 2; x = x_hi * 2 + x_lo), y: 4, z: 16, core: 2. Of those that a mesh axis runs over, the one named last changes fastest.
Arguments:
- rows: float32 [64, 2048, 128], P('rep', 'blk'), may hold values from -6 to 6
- state: float32 [64, 2048], P('rep', 'blk'), may hold values from 1e-09 to 0.001
- bag_ids: int32 [64, 2048, 16], P('rep', 'blk'), may hold values from 0 to 255
- bag_counts: int32 [64, 2048], P('rep', 'blk'), may hold values from 1 to 16
- item_feats: bfloat16 [64, 2048, 128], P('rep', 'blk'), may hold values from -6 to 6
- positives: int32 [64, 2048], P('rep', 'blk'), may hold values from 0 to 2047
- q_w1: bfloat16 [128, 1024], replicated, may hold values from -0.5 to 0.5
- q_w2: bfloat16 [1024, 128], replicated, may hold values from -0.1875 to 0.1875
- i_w1: bfloat16 [128, 1024], replicated, may hold values from -0.5 to 0.5
- i_w2: bfloat16 [1024, 128], replicated, may hold values from -0.1875 to 0.1875
Outputs:
- new_rows: float32 [64, 2048, 128], P('rep', 'blk')
- grad_q1: float32 [128, 1024], replicated
- grad_q2: float32 [1024, 128], replicated
- grad_i1: float32 [128, 1024], replicated
- grad_i2: float32 [1024, 128], replicated
The draws below stay inside these ranges and needn't reach their ends.
All inputs are finite; a program needn't handle non-finite values.
Results may differ from the reference program's by a relative error of at most 0.003.
Values may be sent and summed in bfloat16 or wider, within the bound.
No kernel may reach another device: no remote copies, remote signals or barrier semaphores. Data moves between devices by JAX's collectives and lax.ppermute only.
A program may use at most 64 MiB of HBM per device.

```python
import math
from functools import partial
import jax
import jax.numpy as jnp
from jax import lax

E = 128
H = 1024
BAG = 16
Q_DEV = 256
I_DEV = 256
R_DEV = 256
N_BLK = 8
N_REP = 64


def set_ends(drawn, key, least, high):
    longest = drawn.shape.index(max(drawn.shape))
    spots = []
    for shift in (0, 1):
        where = [jax.random.randint(jax.random.fold_in(key, axis), (), 0, length) for axis, length in enumerate(drawn.shape)]
        where[longest] = (where[longest] + shift) % drawn.shape[longest]
        spots.append(tuple(where))
    return drawn.at[spots[0]].set(least).at[spots[1]].set(high)


def levels(rng, dims, split, least, top_value):
    level, own = 1.0, jax.random.fold_in(rng, 6)
    for axis_at, shards_of in split:
        heights = jnp.exp(jax.random.uniform(jax.random.fold_in(own, axis_at), (shards_of,), jnp.float32, least / len(split), top_value / len(split)))
        level = level * jnp.repeat(heights, dims[axis_at] // shards_of).reshape([-1 if axis == axis_at else 1 for axis in range(len(dims))])
    return level


def scatter_about(own_key, shape, width, bound, pieces=(), kind=jnp.bfloat16):
    level = levels(own_key, shape, pieces, -0.22, 0.18) if pieces else 1.0
    values = jax.random.normal(own_key, shape, jnp.float32) * width * level
    return jnp.minimum(jnp.maximum(values, -bound), bound).astype(kind)


def setup_inputs(seed: int = 0) -> dict:
    key_of = jax.random.split(jax.random.key(seed), 11)
    rows = scatter_about(key_of[0], (N_REP, N_BLK * R_DEV, E), 1.0, 6.0, ((0, 64), (1, 8)), jnp.float32)
    state = jnp.clip(jnp.exp(math.log(0.001) - 13.815511 * jax.random.uniform(key_of[1], (N_REP, N_BLK * R_DEV), jnp.float32) ** levels(key_of[1], (N_REP, N_BLK * R_DEV), ((0, 64), (1, 8)), -0.2, 0.2)), 9.999999717180685e-10, 0.001)
    bag_ids = set_ends(jax.random.randint(key_of[2], (N_REP, N_BLK * Q_DEV, BAG), 0, R_DEV), jax.random.fold_in(key_of[2], 1), 0, R_DEV - 1).astype(jnp.int32)
    bag_counts = set_ends(jax.random.randint(key_of[3], (N_REP, N_BLK * Q_DEV), 1, BAG + 1), jax.random.fold_in(key_of[3], 1), 1, BAG).astype(jnp.int32)
    item_feats = scatter_about(key_of[4], (N_REP, N_BLK * I_DEV, E), 1.0, 6.0, ((0, 64), (1, 8)))
    positives = set_ends(jax.random.randint(key_of[5], (N_REP, N_BLK * Q_DEV), 0, N_BLK * I_DEV), jax.random.fold_in(key_of[5], 1), 0, (N_BLK * I_DEV) - 1).astype(jnp.int32)
    q_w1 = scatter_about(key_of[6], (E, H), E ** -0.5, 0.5)
    q_w2 = scatter_about(key_of[7], (H, E), H ** -0.5, 0.1875)
    i_w1 = scatter_about(key_of[8], (E, H), E ** -0.5, 0.5)
    i_w2 = scatter_about(key_of[9], (H, E), H ** -0.5, 0.1875)
    return dict(rows=rows, state=state, bag_ids=bag_ids, bag_counts=bag_counts, item_feats=item_feats, positives=positives, q_w1=q_w1, q_w2=q_w2, i_w1=i_w1, i_w2=i_w2)


LOGIT_SCALE = 20.0
LEARNING_RATE = 0.5
NORM_EPS = 1e-06

def contract_lead(left, right, precision=None):
    return lax.dot_general(left, right, (((0,), (0,)), ((), ())), precision=precision, preferred_element_type=jnp.float32)

def contract_last(left, right):
    return lax.dot_general(left, right, (((1,), (1,)), ((), ())), preferred_element_type=jnp.float32)

def pooling_matrix(member_ids, member_counts, table_rows):
    columns = lax.broadcasted_iota(jnp.int32, (1, table_rows), 1)
    tally = jnp.zeros((member_ids.shape[0], table_rows), jnp.float32)
    for member in range(member_ids.shape[1]):
        live = (member < member_counts)[:, None]
        tally = tally + jnp.where((member_ids[:, member:member + 1] == columns) & live, 1.0, 0.0)
    return tally / member_counts[:, None].astype(jnp.float32)

def tower(inputs_b, first, second):
    pre = jnp.dot(inputs_b, first, preferred_element_type=jnp.float32)
    hidden = jax.nn.silu(pre).astype(jnp.bfloat16)
    outer = jnp.dot(hidden, second, preferred_element_type=jnp.float32)
    radius = jnp.sqrt(lax.optimization_barrier(jnp.sum(outer * outer, axis=1, keepdims=True)) + NORM_EPS)
    return (pre, hidden, radius, outer / radius)

def tower_back(inputs_b, first, second, pre, hidden, radius, unit, d_unit):
    d_outer = ((d_unit - unit * lax.optimization_barrier(jnp.sum(unit * d_unit, axis=1, keepdims=True))) / radius).astype(jnp.bfloat16)
    grad_second = contract_lead(hidden, d_outer)
    d_hidden = contract_last(d_outer, second)
    sigma = jax.nn.sigmoid(pre)
    d_pre = (d_hidden * sigma * (1.0 + pre * (1.0 - sigma))).astype(jnp.bfloat16)
    grad_first = contract_lead(inputs_b, d_pre)
    d_inputs = contract_last(d_pre, first)
    return (grad_first, grad_second, d_inputs)

def reference(rows, state, bag_ids, bag_counts, item_feats, positives, q_w1, q_w2, i_w1, i_w2):
    norm_c = 1.0 / (Q_DEV * N_BLK)
    build = partial(pooling_matrix, table_rows=R_DEV)

    def group_step(carry, inputs):
        rows_g, state_g, ids_g, counts_g, feats_g, targets_g = inputs
        table = rows_g.reshape(N_BLK, R_DEV, E)
        pools = jax.vmap(build)(ids_g.reshape(N_BLK, Q_DEV, BAG), counts_g.reshape(N_BLK, Q_DEV))
        pooled = jax.vmap(lambda left, right: jnp.dot(left, right, precision=lax.Precision.HIGHEST, preferred_element_type=jnp.float32))(pools, table)
        pooled_b = pooled.reshape(N_BLK * Q_DEV, E).astype(jnp.bfloat16)
        q_pre, q_hidden, q_radius, q_unit = tower(pooled_b, q_w1, q_w2)
        k_pre, k_hidden, k_radius, k_unit = tower(feats_g, i_w1, i_w2)
        queries = q_unit.astype(jnp.bfloat16)
        keys = k_unit.astype(jnp.bfloat16)
        scores = LOGIT_SCALE * contract_last(queries, keys)
        log_total = jnp.log(lax.optimization_barrier(jnp.sum(jnp.exp(scores), axis=1)))
        columns = jnp.arange(N_BLK * I_DEV, dtype=jnp.int32)
        hits = jnp.where(targets_g[:, None] == columns[None, :], 1.0, 0.0)
        weights_b = ((jnp.exp(scores - log_total[:, None]) - hits) * norm_c).astype(jnp.bfloat16)
        d_queries = LOGIT_SCALE * jnp.dot(weights_b, keys, preferred_element_type=jnp.float32)
        d_keys = LOGIT_SCALE * contract_lead(weights_b, queries)
        gq1, gq2, d_pooled = tower_back(pooled_b, q_w1, q_w2, q_pre, q_hidden, q_radius, q_unit, d_queries)
        gi1, gi2, unused = tower_back(feats_g, i_w1, i_w2, k_pre, k_hidden, k_radius, k_unit, d_keys)
        row_grads = jax.vmap(lambda left, right: contract_lead(left, right, lax.Precision.HIGHEST))(pools, d_pooled.reshape(N_BLK, Q_DEV, E))
        row_grads = row_grads.reshape(N_BLK * R_DEV, E)
        accum = state_g + lax.optimization_barrier(jnp.mean(row_grads * row_grads, axis=1))
        updated = rows_g - LEARNING_RATE * row_grads / jnp.sqrt(accum)[:, None]
        carry = (carry[0] + gq1, carry[1] + gq2, carry[2] + gi1, carry[3] + gi2)
        return (carry, updated)
    start = (jnp.zeros((E, H), jnp.float32), jnp.zeros((H, E), jnp.float32), jnp.zeros((E, H), jnp.float32), jnp.zeros((H, E), jnp.float32))
    sums, new_rows = lax.scan(group_step, start, (rows, state, bag_ids, bag_counts, item_feats, positives))
    return (new_rows, sums[0], sums[1], sums[2], sums[3])
```

```python
import functools

import jax
import jax.numpy as jnp
from jax import lax
from jax.experimental import pallas as pl
from jax.experimental.pallas import tpu as pltpu
from jax.sharding import Mesh, PartitionSpec as P

LOGIT_SCALE = 20.0
LEARNING_RATE = 0.5
NORM_EPS = 1e-06

BF16 = jnp.bfloat16
F32 = jnp.float32

CODE_ROWS = 16
LANES = 128


def contract_lead(left, right):
    return lax.dot_general(left, right, (((0,), (0,)), ((), ())), preferred_element_type=F32)


def contract_last(left, right):
    return lax.dot_general(left, right, (((1,), (1,)), ((), ())), preferred_element_type=F32)


def column_of(row):
    return jnp.transpose(jnp.broadcast_to(row, (LANES, row.shape[1])))


def three_pieces(values):
    high = values.astype(BF16)
    rest = values - high.astype(F32)
    middle = rest.astype(BF16)
    low = (rest - middle.astype(F32)).astype(BF16)
    return jnp.concatenate([high, middle, low], axis=1)


def add_pieces(product):
    return (product[:, 2 * LANES :] + product[:, LANES : 2 * LANES]) + product[:, :LANES]


def front_kernel(
    ids_ref, counts_ref, pos_ref, table_ref, feats_ref, qw1_ref, qw2_ref, iw1_ref, iw2_ref,
    payload_ref, pooled_ref, tally_ref, units_ref, radii_ref,
):
    q_rows, members = ids_ref.shape
    table_rows = table_ref.shape[0]
    counts = column_of(counts_ref[...].astype(F32))
    member = lax.broadcasted_iota(jnp.int32, (q_rows, members), 1).astype(F32)
    ids = jnp.where(member < counts[:, :members], ids_ref[...], -1)
    columns = lax.broadcasted_iota(jnp.int32, (q_rows, table_rows), 1)
    tally = jnp.zeros((q_rows, table_rows), F32)
    for m in range(members):
        tally = tally + jnp.where(ids[:, m : m + 1] == columns, 1.0, 0.0)
    tally = tally.astype(BF16)
    tally_ref[...] = tally
    product = jnp.dot(tally, three_pieces(table_ref[...]), preferred_element_type=F32)
    pooled = (add_pieces(product) / counts).astype(BF16)
    pooled_ref[...] = pooled

    def tower(inputs, first_ref, second_ref, slot):
        pre = jnp.dot(inputs, first_ref[...], preferred_element_type=F32)
        hidden = (pre * jax.nn.sigmoid(pre)).astype(BF16)
        outer = jnp.dot(hidden, second_ref[...], preferred_element_type=F32)
        radius = jnp.sqrt(jnp.sum(outer * outer, axis=1, keepdims=True) + NORM_EPS)
        unit = outer / radius
        units_ref[slot] = unit
        radii_ref[slot] = jnp.broadcast_to(radius, unit.shape)
        return unit.astype(BF16)

    keys = tower(feats_ref[...], iw1_ref, iw2_ref, 1)
    queries = tower(pooled, qw1_ref, qw2_ref, 0)
    pos = pos_ref[...]
    digits = jnp.concatenate([pos // LANES, pos % LANES], axis=0).astype(F32)
    spread = jnp.concatenate(
        [digits[:, i * LANES : (i + 1) * LANES] for i in range(q_rows // LANES)]
        + [jnp.zeros((CODE_ROWS - 2 * (q_rows // LANES), LANES), F32)],
        axis=0,
    ).astype(BF16)
    for copy in range(payload_ref.shape[0]):
        payload_ref[copy, :q_rows] = queries
        payload_ref[copy, q_rows : 2 * q_rows] = keys
        payload_ref[copy, 2 * q_rows :] = spread


def middle_kernel(
    where_ref, all_ref, pos_ref, pooled_ref, feats_ref, units_ref, radii_ref,
    qw1_ref, qw2_ref, iw1_ref, iw2_ref,
    keep_ref, send_ref, d_x_ref,
    totals_ref, codes_ref, d_units_ref, grads_ref,
):
    ranks = all_ref.shape[0]
    q_rows = pooled_ref.shape[0]
    i_rows = feats_ref.shape[0]
    blk = where_ref[0]
    core = where_ref[1]
    norm_c = 1.0 / (q_rows * ranks)

    def add_group(s, carry):
        queries = all_ref[s, :q_rows]
        partial = jnp.zeros((8, q_rows), F32)
        for t in range(ranks):
            scores = LOGIT_SCALE * contract_last(all_ref[t, q_rows : q_rows + i_rows], queries)
            partial = partial + jnp.sum(jnp.exp(scores).reshape(i_rows // 8, 8, q_rows), axis=0)
        totals_ref[s] = jnp.broadcast_to(jnp.sum(partial, axis=0, keepdims=True), (8, q_rows))
        digits = all_ref[s, q_rows + i_rows :].astype(F32)
        chunks = q_rows // LANES
        code = jnp.concatenate(
            [digits[2 * i : 2 * i + 1] * LANES + digits[2 * i + 1 : 2 * i + 2] for i in range(chunks)],
            axis=1,
        )
        codes_ref[s] = jnp.broadcast_to(code.astype(jnp.int32), (8, q_rows))
        return carry

    lax.fori_loop(0, ranks, add_group, 0)

    own_keys = all_ref[blk, q_rows : q_rows + i_rows]
    item = blk * i_rows + lax.broadcasted_iota(jnp.int32, (i_rows, q_rows), 0)
    d_keys = jnp.zeros((i_rows, LANES), F32)
    for s in range(ranks):
        queries = all_ref[s, :q_rows]
        shares = jnp.exp(LOGIT_SCALE * contract_last(own_keys, queries)) * (1.0 / totals_ref[s, :1])
        hits = jnp.where(codes_ref[s, :1] == item, 1.0, 0.0)
        weights = ((shares - hits) * norm_c).astype(BF16)
        d_keys = d_keys + jnp.dot(weights, queries, preferred_element_type=F32)
    d_units_ref[1] = LOGIT_SCALE * d_keys

    own_queries = all_ref[blk, :q_rows]
    total = column_of(totals_ref[blk, :1])
    inverse = jnp.concatenate([1.0 / total] * (i_rows // LANES), axis=1)
    target = jnp.concatenate([column_of(pos_ref[...])] * (i_rows // LANES), axis=1)
    place = lax.broadcasted_iota(jnp.int32, (q_rows, i_rows), 1)
    d_queries = jnp.zeros((q_rows, LANES), F32)
    for t in range(ranks):
        keys = all_ref[t, q_rows : q_rows + i_rows]
        shares = jnp.exp(LOGIT_SCALE * contract_last(own_queries, keys)) * inverse
        hits = jnp.where(target == place + t * i_rows, 1.0, 0.0)
        weights = ((shares - hits) * norm_c).astype(BF16)
        d_queries = d_queries + jnp.dot(weights, keys, preferred_element_type=F32)
    d_units_ref[0] = LOGIT_SCALE * d_queries

    def tower_back(inputs, first_ref, second_ref, slot):
        unit = units_ref[slot]
        d_unit = d_units_ref[slot]
        along = jnp.sum(unit * d_unit, axis=1, keepdims=True)
        d_outer = ((d_unit - unit * along) / radii_ref[slot]).astype(BF16)
        pre = jnp.dot(inputs, first_ref[...], preferred_element_type=F32)
        sigma = jax.nn.sigmoid(pre)
        hidden = (pre * sigma).astype(BF16)
        h = hidden.shape[1]
        grads_ref[slot, h:] = contract_lead(hidden, d_outer)
        d_hidden = contract_last(d_outer, second_ref[...])
        d_pre = (d_hidden * sigma * (1.0 + pre * (1.0 - sigma))).astype(BF16)
        first_grad = contract_lead(inputs, d_pre)
        for i in range(h // LANES):
            grads_ref[slot, i * LANES : (i + 1) * LANES] = first_grad[:, i * LANES : (i + 1) * LANES]
        return d_pre

    tower_back(feats_ref[...], iw1_ref, iw2_ref, 1)
    d_pre = tower_back(pooled_ref[...], qw1_ref, qw2_ref, 0)
    d_x_ref[...] = contract_last(d_pre, qw1_ref[...])
    keep_ref[...] = grads_ref[core]
    send_ref[...] = grads_ref[1 - core].astype(BF16)


def rows_kernel(tally_ref, counts_ref, d_x_ref, table_ref, state_ref, new_ref):
    counts = column_of(counts_ref[...].astype(F32))
    pieces = three_pieces(d_x_ref[...] / counts)
    row_grads = add_pieces(contract_lead(tally_ref[...], pieces))
    mean = jnp.mean(row_grads * row_grads, axis=1, keepdims=True)
    acc = column_of(state_ref[...]) + mean
    new_ref[...] = table_ref[...] - LEARNING_RATE * row_grads / jnp.sqrt(acc)


def finish_kernel(where_ref, mine_ref, other_ref, q1_ref, q2_ref, i1_ref, i2_ref):
    core = where_ref[1]
    h = q2_ref.shape[0]

    def write(source_ref, first_ref, second_ref):
        for i in range(h // LANES):
            first_ref[:, i * LANES : (i + 1) * LANES] = source_ref[i * LANES : (i + 1) * LANES].astype(F32)
        second_ref[...] = source_ref[h:].astype(F32)

    @pl.when(core == 0)
    def _():
        write(mine_ref, q1_ref, q2_ref)
        write(other_ref, i1_ref, i2_ref)

    @pl.when(core != 0)
    def _():
        write(other_ref, q1_ref, q2_ref)
        write(mine_ref, i1_ref, i2_ref)


VMEM = pl.BlockSpec(memory_space=pltpu.VMEM)
SMEM = pl.BlockSpec(memory_space=pltpu.SMEM)


def call(kernel, out_shape, operands, scalars=0, scratch=(), flops=0, limit=32):
    return pl.pallas_call(
        kernel,
        out_shape=out_shape,
        in_specs=[SMEM] * scalars + [VMEM] * (len(operands) - scalars),
        out_specs=jax.tree.map(lambda _: VMEM, out_shape),
        scratch_shapes=list(scratch),
        compiler_params=pltpu.CompilerParams(vmem_limit_bytes=limit * 2**20),
        cost_estimate=pl.CostEstimate(flops=flops, bytes_accessed=4 * 2**20, transcendentals=0),
    )(*operands)


def exchange(values, axes):
    return lax.all_to_all(values, axes, 0, 0, tiled=True)


def gather_sum(values, axis):
    copies = jnp.broadcast_to(values, (lax.axis_size(axis),) + values.shape)
    return jnp.sum(exchange(copies, axis), axis=0)


def per_device(rows, state, bag_ids, bag_counts, item_feats, positives, q_w1, q_w2, i_w1, i_w2):
    group = ("y", "xl")
    plane = ("y", "xl", "xh")
    struct = jax.ShapeDtypeStruct
    ranks = lax.axis_size(group)
    chips = lax.axis_size(plane)
    table = rows[0]
    feats = item_feats[0]
    q_rows, e = bag_ids.shape[1], table.shape[1]
    i_rows = feats.shape[0]
    h = q_w2.shape[0]
    where = jnp.stack([lax.axis_index(group), lax.axis_index("c")]).astype(jnp.int32)

    payload, pooled, tally, units, radii = call(
        front_kernel,
        [
            struct((ranks, q_rows + i_rows + CODE_ROWS, e), BF16),
            struct((q_rows, e), BF16),
            struct((q_rows, table.shape[0]), BF16),
            struct((2, q_rows, e), F32),
            struct((2, q_rows, e), F32),
        ],
        [bag_ids[0], bag_counts, positives, table, feats, q_w1, q_w2, i_w1, i_w2],
    )
    everyone = exchange(payload, group)
    keep, send, d_x = call(
        middle_kernel,
        [struct((2 * h, e), F32), struct((2 * h, e), BF16), struct((q_rows, e), F32)],
        [where, everyone, positives, pooled, feats, units, radii, q_w1, q_w2, i_w1, i_w2],
        scalars=1,
        scratch=[
            pltpu.VMEM((ranks, 8, q_rows), F32),
            pltpu.VMEM((ranks, 8, q_rows), jnp.int32),
            pltpu.VMEM((2, q_rows, e), F32),
            pltpu.VMEM((2, 2 * h, e), F32),
        ],
    )
    swap = [(0, 1), (1, 0)]
    received = lax.ppermute(send, "c", swap)
    new_rows = call(
        rows_kernel, struct(table.shape, F32), [tally, bag_counts, d_x, table, state], flops=2**27
    )
    chip_sum = (keep + received.astype(F32)).astype(BF16).reshape(chips, 2 * h // chips, e)
    mine = jnp.sum(exchange(chip_sum, plane).astype(F32), axis=0)
    mine = gather_sum(mine, "zl")
    mine = gather_sum(mine, "zh")
    copies = jnp.broadcast_to(mine.astype(BF16), (chips,) + mine.shape)
    tower = exchange(copies, plane).reshape(2 * h, e)
    other = lax.ppermute(tower, "c", swap)
    sums = call(
        finish_kernel,
        [struct((e, h), F32), struct((h, e), F32), struct((e, h), F32), struct((h, e), F32)],
        [where, tower, other],
        scalars=1,
    )
    return (new_rows[None], *sums)


def solution(mesh):
    blk, rep = mesh.devices.shape
    strided = 4 if rep % 16 == 0 else 1
    parts = (blk // 2, 2, strided, rep // (strided * 4) if rep >= 4 else 1, 2 if rep >= 4 else 1, 2)
    fine = Mesh(mesh.devices.reshape(parts), ("y", "xl", "zh", "zl", "xh", "c"))
    rep_axes = ("zh", "zl", "xh", "c")
    blk_axes = ("y", "xl")
    in_specs = (
        P(rep_axes, blk_axes, None),
        P(rep_axes, blk_axes),
        P(rep_axes, blk_axes, None),
        P(rep_axes, blk_axes),
        P(rep_axes, blk_axes, None),
        P(rep_axes, blk_axes),
        P(),
        P(),
        P(),
        P(),
    )
    out_specs = (P(rep_axes, blk_axes, None), P(), P(), P(), P())
    return jax.shard_map(
        per_device, mesh=fine, in_specs=in_specs, out_specs=out_specs, check_vma=False
    )
```

```python
import functools

import jax
import jax.numpy as jnp
from jax import lax
from jax.experimental import pallas as pl
from jax.experimental.pallas import tpu as pltpu
from jax.sharding import Mesh, PartitionSpec as P

LOGIT_SCALE = 20.0
LEARNING_RATE = 0.5
NORM_EPS = 1e-06

BF16 = jnp.bfloat16
F32 = jnp.float32

CODE_ROWS = 16
LANES = 128


def contract_lead(left, right):
    return lax.dot_general(left, right, (((0,), (0,)), ((), ())), preferred_element_type=F32)


def contract_last(left, right):
    return lax.dot_general(left, right, (((1,), (1,)), ((), ())), preferred_element_type=F32)


def column_of(row):
    return jnp.transpose(jnp.broadcast_to(row, (LANES, row.shape[1])))


def three_pieces(values):
    high = values.astype(BF16)
    rest = values - high.astype(F32)
    middle = rest.astype(BF16)
    low = (rest - middle.astype(F32)).astype(BF16)
    return jnp.concatenate([high, middle, low], axis=1)


def add_pieces(product):
    return (product[:, 2 * LANES :] + product[:, LANES : 2 * LANES]) + product[:, :LANES]


def front_kernel(
    ids_hbm, counts_hbm, pos_hbm, table_hbm, feats_hbm, qw1_hbm, qw2_hbm, iw1_hbm, iw2_hbm,
    payload_ref, pooled_ref, tally_ref, units_ref, radii_ref,
    ids_ref, counts_ref, pos_ref, table_ref, feats_ref, qw1_ref, qw2_ref, iw1_ref, iw2_ref, arrived,
):
    sources = (ids_hbm, counts_hbm, table_hbm, qw1_hbm, feats_hbm, iw1_hbm, qw2_hbm, iw2_hbm, pos_hbm)
    targets = (ids_ref, counts_ref, table_ref, qw1_ref, feats_ref, iw1_ref, qw2_ref, iw2_ref, pos_ref)
    copies = [
        pltpu.make_async_copy(source, target, arrived.at[i])
        for i, (source, target) in enumerate(zip(sources, targets))
    ]
    for copy in copies:
        copy.start()

    members, q_rows = ids_ref.shape
    table_rows = table_ref.shape[0]
    copies[0].wait()
    copies[1].wait()
    counts = counts_ref[...]
    rows = lax.broadcasted_iota(jnp.int32, (table_rows, q_rows), 0)
    tally = jnp.zeros((table_rows, q_rows), F32)
    for m in range(members):
        live = jnp.where(counts > m, ids_ref[m : m + 1], -1)
        tally = tally + jnp.where(live == rows, 1.0, 0.0)
    tally = tally.astype(BF16)
    tally_ref[...] = tally
    copies[2].wait()
    product = contract_lead(tally, three_pieces(table_ref[...]))
    pooled = (add_pieces(product) / column_of(counts.astype(F32))).astype(BF16)
    pooled_ref[...] = pooled

    def tower(inputs, first, second, slot):
        copies[first].wait()
        pre = jnp.dot(inputs, targets[first][...], preferred_element_type=F32)
        hidden = (pre * jax.nn.sigmoid(pre)).astype(BF16)
        copies[second].wait()
        outer = jnp.dot(hidden, targets[second][...], preferred_element_type=F32)
        radius = jnp.sqrt(jnp.sum(outer * outer, axis=1, keepdims=True) + NORM_EPS)
        unit = outer / radius
        units_ref[slot] = unit
        radii_ref[slot] = jnp.broadcast_to(radius, unit.shape)
        return unit.astype(BF16)

    queries = tower(pooled, 3, 6, 0)
    copies[4].wait()
    keys = tower(feats_ref[...], 5, 7, 1)
    copies[8].wait()
    pos = pos_ref[...]
    digits = jnp.concatenate([pos // LANES, pos % LANES], axis=0).astype(F32)
    spread = jnp.concatenate(
        [digits[:, i * LANES : (i + 1) * LANES] for i in range(q_rows // LANES)]
        + [jnp.zeros((CODE_ROWS - 2 * (q_rows // LANES), LANES), F32)],
        axis=0,
    ).astype(BF16)
    for copy in range(payload_ref.shape[0]):
        payload_ref[copy, :q_rows] = queries
        payload_ref[copy, q_rows : 2 * q_rows] = keys
        payload_ref[copy, 2 * q_rows :] = spread


def middle_kernel(
    where_ref, all_ref, pos_ref, pooled_ref, feats_ref, units_ref, radii_ref,
    qw1_ref, qw2_ref, iw1_ref, iw2_ref,
    keep_ref, send_ref, d_x_ref,
    totals_ref, codes_ref, d_units_ref, grads_ref,
):
    ranks = all_ref.shape[0]
    q_rows = pooled_ref.shape[0]
    i_rows = feats_ref.shape[0]
    blk = where_ref[0]
    core = where_ref[1]
    norm_c = 1.0 / (q_rows * ranks)

    def add_group(s, carry):
        queries = all_ref[s, :q_rows]
        partial = jnp.zeros((8, q_rows), F32)
        for t in range(ranks):
            scores = LOGIT_SCALE * contract_last(all_ref[t, q_rows : q_rows + i_rows], queries)
            partial = partial + jnp.sum(jnp.exp(scores).reshape(i_rows // 8, 8, q_rows), axis=0)
        totals_ref[s] = jnp.broadcast_to(jnp.sum(partial, axis=0, keepdims=True), (8, q_rows))
        digits = all_ref[s, q_rows + i_rows :].astype(F32)
        chunks = q_rows // LANES
        code = jnp.concatenate(
            [digits[2 * i : 2 * i + 1] * LANES + digits[2 * i + 1 : 2 * i + 2] for i in range(chunks)],
            axis=1,
        )
        codes_ref[s] = jnp.broadcast_to(code.astype(jnp.int32), (8, q_rows))
        return carry

    lax.fori_loop(0, ranks, add_group, 0)

    own_keys = all_ref[blk, q_rows : q_rows + i_rows]
    item = blk * i_rows + lax.broadcasted_iota(jnp.int32, (i_rows, q_rows), 0)
    d_keys = jnp.zeros((i_rows, LANES), F32)
    for s in range(ranks):
        queries = all_ref[s, :q_rows]
        shares = jnp.exp(LOGIT_SCALE * contract_last(own_keys, queries)) * (1.0 / totals_ref[s, :1])
        hits = jnp.where(codes_ref[s, :1] == item, 1.0, 0.0)
        weights = ((shares - hits) * norm_c).astype(BF16)
        d_keys = d_keys + jnp.dot(weights, queries, preferred_element_type=F32)
    d_units_ref[1] = LOGIT_SCALE * d_keys

    own_queries = all_ref[blk, :q_rows]
    total = column_of(totals_ref[blk, :1])
    inverse = jnp.concatenate([1.0 / total] * (i_rows // LANES), axis=1)
    target = jnp.concatenate([column_of(pos_ref[...])] * (i_rows // LANES), axis=1)
    place = lax.broadcasted_iota(jnp.int32, (q_rows, i_rows), 1)
    d_queries = jnp.zeros((q_rows, LANES), F32)
    for t in range(ranks):
        keys = all_ref[t, q_rows : q_rows + i_rows]
        shares = jnp.exp(LOGIT_SCALE * contract_last(own_queries, keys)) * inverse
        hits = jnp.where(target == place + t * i_rows, 1.0, 0.0)
        weights = ((shares - hits) * norm_c).astype(BF16)
        d_queries = d_queries + jnp.dot(weights, keys, preferred_element_type=F32)
    d_units_ref[0] = LOGIT_SCALE * d_queries

    def tower_back(inputs, first_ref, second_ref, slot):
        unit = units_ref[slot]
        d_unit = d_units_ref[slot]
        along = jnp.sum(unit * d_unit, axis=1, keepdims=True)
        d_outer = ((d_unit - unit * along) / radii_ref[slot]).astype(BF16)
        pre = jnp.dot(inputs, first_ref[...], preferred_element_type=F32)
        sigma = jax.nn.sigmoid(pre)
        hidden = (pre * sigma).astype(BF16)
        h = hidden.shape[1]
        grads_ref[slot, h:] = contract_lead(hidden, d_outer)
        d_hidden = contract_last(d_outer, second_ref[...])
        d_pre = (d_hidden * sigma * (1.0 + pre * (1.0 - sigma))).astype(BF16)
        first_grad = contract_lead(inputs, d_pre)
        for i in range(h // LANES):
            grads_ref[slot, i * LANES : (i + 1) * LANES] = first_grad[:, i * LANES : (i + 1) * LANES]
        return d_pre

    tower_back(feats_ref[...], iw1_ref, iw2_ref, 1)
    d_pre = tower_back(pooled_ref[...], qw1_ref, qw2_ref, 0)
    d_x_ref[...] = contract_last(d_pre, qw1_ref[...])
    keep_ref[...] = grads_ref[core]
    send_ref[...] = grads_ref[1 - core].astype(BF16)


def rows_kernel(tally_ref, counts_ref, d_x_ref, table_ref, state_ref, new_ref):
    counts = column_of(counts_ref[...].astype(F32))
    pieces = three_pieces(d_x_ref[...] / counts)
    row_grads = add_pieces(jnp.dot(tally_ref[...], pieces, preferred_element_type=F32))
    mean = jnp.mean(row_grads * row_grads, axis=1, keepdims=True)
    acc = column_of(state_ref[...]) + mean
    new_ref[...] = table_ref[...] - LEARNING_RATE * row_grads / jnp.sqrt(acc)


def finish_kernel(mine, where_ref, source_ref, *refs):
    q1_ref, q2_ref, i1_ref, i2_ref, first_ref, second_ref, sent = refs[-7:]
    core = where_ref[1]
    e, h = first_ref.shape

    def copies(first_hbm, second_hbm):
        return [
            pltpu.make_async_copy(first_ref, first_hbm, sent.at[0]),
            pltpu.make_async_copy(second_ref, second_hbm, sent.at[1]),
        ]

    def write(first_hbm, second_hbm):
        first, second = copies(first_hbm, second_hbm)
        second_ref[...] = source_ref[h:].astype(F32)
        second.start()
        for i in range(h // LANES):
            first_ref[:, i * LANES : (i + 1) * LANES] = source_ref[i * LANES : (i + 1) * LANES].astype(F32)
        first.start()
        second.wait()
        first.wait()

    query_tower = (core == 0) if mine else (core != 0)

    @pl.when(query_tower)
    def _():
        write(q1_ref, q2_ref)

    @pl.when(jnp.logical_not(query_tower))
    def _():
        write(i1_ref, i2_ref)


VMEM = pl.BlockSpec(memory_space=pltpu.VMEM)
SMEM = pl.BlockSpec(memory_space=pltpu.SMEM)
HBM = pl.BlockSpec(memory_space=pltpu.HBM)


def call(kernel, out_shape, operands, in_specs=None, out_specs=None, scratch=(), flops=0, limit=32, aliases=None):
    return pl.pallas_call(
        kernel,
        out_shape=out_shape,
        in_specs=in_specs or [VMEM] * len(operands),
        out_specs=out_specs or jax.tree.map(lambda _: VMEM, out_shape),
        scratch_shapes=list(scratch),
        input_output_aliases=aliases or {},
        compiler_params=pltpu.CompilerParams(vmem_limit_bytes=limit * 2**20),
        cost_estimate=pl.CostEstimate(flops=flops, bytes_accessed=2**20, transcendentals=0),
    )(*operands)


def exchange(values, axes):
    return lax.all_to_all(values, axes, 0, 0, tiled=True)


def per_device(rows, state, bag_ids, bag_counts, item_feats, positives, q_w1, q_w2, i_w1, i_w2):
    group = ("y", "xl")
    block = ("y", "xl", "zp", "xh")
    struct = jax.ShapeDtypeStruct
    ranks = lax.axis_size(group)
    spread = lax.axis_size(block)
    table = rows[0]
    feats = item_feats[0]
    q_rows, e = bag_ids.shape[1], table.shape[1]
    i_rows = feats.shape[0]
    h = q_w2.shape[0]
    where = jnp.stack([lax.axis_index(group), lax.axis_index("c")]).astype(jnp.int32)

    ids = bag_ids[0].T
    arguments = [ids, bag_counts, positives, table, feats, q_w1, q_w2, i_w1, i_w2]
    payload, pooled, tally, units, radii = call(
        front_kernel,
        [
            struct((ranks, q_rows + i_rows + CODE_ROWS, e), BF16),
            struct((q_rows, e), BF16),
            struct((table.shape[0], q_rows), BF16),
            struct((2, q_rows, e), F32),
            struct((2, q_rows, e), F32),
        ],
        arguments,
        in_specs=[HBM] * len(arguments),
        scratch=[pltpu.VMEM(a.shape, a.dtype) for a in arguments]
        + [pltpu.SemaphoreType.DMA((len(arguments),))],
    )
    everyone = exchange(payload, group)
    keep, send, d_x = call(
        middle_kernel,
        [struct((2 * h, e), F32), struct((2 * h, e), BF16), struct((q_rows, e), F32)],
        [where, everyone, positives, pooled, feats, units, radii, q_w1, q_w2, i_w1, i_w2],
        in_specs=[SMEM] + [VMEM] * 10,
        scratch=[
            pltpu.VMEM((ranks, 8, q_rows), F32),
            pltpu.VMEM((ranks, 8, q_rows), jnp.int32),
            pltpu.VMEM((2, q_rows, e), F32),
            pltpu.VMEM((2, 2 * h, e), F32),
        ],
    )
    swap = [(0, 1), (1, 0)]
    received = lax.ppermute(send, "c", swap)
    new_rows = call(
        rows_kernel, struct(table.shape, F32), [tally, bag_counts, d_x, table, state], flops=2**30
    )
    chip_sum = (keep + received.astype(F32)).astype(BF16).reshape(spread, 2 * h // spread, e)
    chip_sum, new_rows = lax.optimization_barrier((chip_sum, new_rows))
    mine = jnp.sum(exchange(chip_sum, block).astype(F32), axis=0).astype(BF16)
    copies = jnp.broadcast_to(mine, (lax.axis_size("zh"),) + mine.shape)
    mine = jnp.sum(exchange(copies, "zh").astype(F32), axis=0).astype(BF16)
    copies = jnp.broadcast_to(mine, (spread,) + mine.shape)
    tower = exchange(copies, block).reshape(2 * h, e)
    other = lax.ppermute(tower, "c", swap)
    shapes = [struct((e, h), F32), struct((h, e), F32), struct((e, h), F32), struct((h, e), F32)]
    buffers = [pltpu.VMEM((e, h), F32), pltpu.VMEM((h, e), F32), pltpu.SemaphoreType.DMA((2,))]
    own = call(
        functools.partial(finish_kernel, True),
        shapes,
        [where, tower],
        in_specs=[SMEM, VMEM],
        out_specs=[HBM] * 4,
        scratch=buffers,
        flops=2**30,
    )
    sums = call(
        functools.partial(finish_kernel, False),
        shapes,
        [where, other, *own],
        in_specs=[SMEM, VMEM] + [HBM] * 4,
        out_specs=[HBM] * 4,
        scratch=buffers,
        aliases={2: 0, 3: 1, 4: 2, 5: 3},
    )
    return (new_rows[None], *sums)


def solution(mesh):
    blk, rep = mesh.devices.shape
    parts = (blk // 2, 2, max(rep // 8, 1), 2 if rep >= 8 else 1, 2 if rep >= 4 else 1, 2)
    fine = Mesh(mesh.devices.reshape(parts), ("y", "xl", "zh", "zp", "xh", "c"))
    rep_axes = ("zh", "zp", "xh", "c")
    blk_axes = ("y", "xl")
    in_specs = (
        P(rep_axes, blk_axes, None),
        P(rep_axes, blk_axes),
        P(rep_axes, blk_axes, None),
        P(rep_axes, blk_axes),
        P(rep_axes, blk_axes, None),
        P(rep_axes, blk_axes),
        P(),
        P(),
        P(),
        P(),
    )
    out_specs = (P(rep_axes, blk_axes, None), P(), P(), P(), P())
    return jax.shard_map(
        per_device, mesh=fine, in_specs=in_specs, out_specs=out_specs, check_vma=False
    )
```

```python
import functools

import jax
import jax.numpy as jnp
from jax import lax
from jax.experimental import pallas as pl
from jax.experimental.pallas import tpu as pltpu
from jax.sharding import Mesh, PartitionSpec as P

LOGIT_SCALE = 20.0
EXP_SCALE = 28.853900817779268
LEARNING_RATE = 0.5
NORM_EPS = 1e-06

BF16 = jnp.bfloat16
F32 = jnp.float32

CODE_ROWS = 16
LANES = 128


def contract_lead(left, right):
    return lax.dot_general(left, right, (((0,), (0,)), ((), ())), preferred_element_type=F32)


def contract_last(left, right):
    return lax.dot_general(left, right, (((1,), (1,)), ((), ())), preferred_element_type=F32)


def column_of(row):
    return jnp.transpose(jnp.broadcast_to(row, (LANES, row.shape[1])))


def three_pieces(values):
    high = values.astype(BF16)
    rest = values - high.astype(F32)
    middle = rest.astype(BF16)
    low = (rest - middle.astype(F32)).astype(BF16)
    return jnp.concatenate([high, middle, low], axis=1)


def add_pieces(product):
    return (product[:, 2 * LANES :] + product[:, LANES : 2 * LANES]) + product[:, :LANES]


def front_kernel(
    ids_hbm, counts_hbm, pos_hbm, table_hbm, feats_hbm, qw1_hbm, qw2_hbm, iw1_hbm, iw2_hbm,
    payload_ref, pooled_ref, tally_ref, units_ref, radii_ref,
    ids_ref, counts_ref, pos_ref, table_ref, feats_ref, qw1_ref, qw2_ref, iw1_ref, iw2_ref, arrived,
):
    sources = (ids_hbm, counts_hbm, table_hbm, qw1_hbm, feats_hbm, iw1_hbm, qw2_hbm, iw2_hbm, pos_hbm)
    targets = (ids_ref, counts_ref, table_ref, qw1_ref, feats_ref, iw1_ref, qw2_ref, iw2_ref, pos_ref)
    copies = [
        pltpu.make_async_copy(source, target, arrived.at[i])
        for i, (source, target) in enumerate(zip(sources, targets))
    ]
    for copy in copies:
        copy.start()

    members, q_rows = ids_ref.shape
    table_rows = table_ref.shape[0]
    copies[0].wait()
    copies[1].wait()
    counts = counts_ref[...]
    rows = lax.broadcasted_iota(jnp.int32, (table_rows, q_rows), 0)
    tally = jnp.zeros((table_rows, q_rows), F32)
    for m in range(members):
        live = jnp.where(counts > m, ids_ref[m : m + 1], -1)
        tally = tally + jnp.where(live == rows, 1.0, 0.0)
    tally = tally.astype(BF16)
    tally_ref[...] = tally
    copies[2].wait()
    product = contract_lead(tally, three_pieces(table_ref[...]))
    pooled = (add_pieces(product) / column_of(counts.astype(F32))).astype(BF16)
    pooled_ref[...] = pooled

    def tower(inputs, first, second, slot):
        copies[first].wait()
        pre = jnp.dot(inputs, targets[first][...], preferred_element_type=F32)
        hidden = (pre * jax.nn.sigmoid(pre)).astype(BF16)
        copies[second].wait()
        outer = jnp.dot(hidden, targets[second][...], preferred_element_type=F32)
        radius = jnp.sqrt(jnp.sum(outer * outer, axis=1, keepdims=True) + NORM_EPS)
        unit = outer / radius
        units_ref[slot] = unit
        radii_ref[slot] = jnp.broadcast_to(radius, unit.shape)
        return unit.astype(BF16)

    queries = tower(pooled, 3, 6, 0)
    copies[4].wait()
    keys = tower(feats_ref[...], 5, 7, 1)
    copies[8].wait()
    pos = pos_ref[...]
    digits = jnp.concatenate([pos // LANES, pos % LANES], axis=0).astype(F32)
    spread = jnp.concatenate(
        [digits[:, i * LANES : (i + 1) * LANES] for i in range(q_rows // LANES)]
        + [jnp.zeros((CODE_ROWS - 2 * (q_rows // LANES), LANES), F32)],
        axis=0,
    ).astype(BF16)
    for copy in range(payload_ref.shape[0]):
        payload_ref[copy, :q_rows] = queries
        payload_ref[copy, q_rows : 2 * q_rows] = keys
        payload_ref[copy, 2 * q_rows :] = spread


def middle_kernel(
    where_ref, all_ref, pos_ref, pooled_ref, feats_ref, units_ref, radii_ref,
    qw1_ref, qw2_ref, iw1_ref, iw2_ref,
    keep_ref, send_ref, d_x_ref,
    totals_ref, codes_ref, d_units_ref, grads_ref,
):
    ranks = all_ref.shape[0]
    q_rows = pooled_ref.shape[0]
    i_rows = feats_ref.shape[0]
    blk = where_ref[0]
    core = where_ref[1]
    norm_c = 1.0 / (q_rows * ranks)

    def add_group(s, carry):
        queries = all_ref[s, :q_rows]

        def add_items(t, partial):
            scores = EXP_SCALE * contract_last(all_ref[t, q_rows : q_rows + i_rows], queries)
            return partial + jnp.sum(jnp.exp2(scores).reshape(i_rows // 8, 8, q_rows), axis=0)

        partial = lax.fori_loop(0, ranks, add_items, jnp.zeros((8, q_rows), F32), unroll=True)
        totals_ref[s] = jnp.broadcast_to(jnp.sum(partial, axis=0, keepdims=True), (8, q_rows))
        digits = all_ref[s, q_rows + i_rows :].astype(F32)
        chunks = q_rows // LANES
        code = jnp.concatenate(
            [digits[2 * i : 2 * i + 1] * LANES + digits[2 * i + 1 : 2 * i + 2] for i in range(chunks)],
            axis=1,
        )
        codes_ref[s] = jnp.broadcast_to(code.astype(jnp.int32), (8, q_rows))
        return carry

    lax.fori_loop(0, ranks, add_group, 0, unroll=True)

    own_keys = all_ref[blk, q_rows : q_rows + i_rows]

    def add_queries(s, d_keys):
        queries = all_ref[s, :q_rows]
        shares = jnp.exp2(EXP_SCALE * contract_last(own_keys, queries)) * (norm_c / totals_ref[s, :1])
        item = blk * i_rows + lax.broadcasted_iota(jnp.int32, (i_rows, q_rows), 0)
        weights = (shares - jnp.where(codes_ref[s, :1] == item, norm_c, 0.0)).astype(BF16)
        return d_keys + jnp.dot(weights, queries, preferred_element_type=F32)


    own_queries = all_ref[blk, :q_rows]
    inverse = column_of(norm_c / totals_ref[blk, :1])
    inverse = jnp.concatenate([inverse] * (i_rows // LANES), axis=1)
    target = jnp.concatenate([column_of(pos_ref[...])] * (i_rows // LANES), axis=1)
    target = target - lax.broadcasted_iota(jnp.int32, (q_rows, i_rows), 1)

    def add_keys(t, d_queries):
        keys = all_ref[t, q_rows : q_rows + i_rows]
        shares = jnp.exp2(EXP_SCALE * contract_last(own_queries, keys)) * inverse
        weights = (shares - jnp.where(target == t * i_rows, norm_c, 0.0)).astype(BF16)
        return d_queries + jnp.dot(weights, keys, preferred_element_type=F32)

    d_keys = jnp.zeros((i_rows, LANES), F32)
    d_queries = jnp.zeros((q_rows, LANES), F32)
    for r in range(ranks):
        d_keys = add_queries(r, d_keys)
        d_queries = add_keys(r, d_queries)
    d_units_ref[1] = LOGIT_SCALE * d_keys
    d_units_ref[0] = LOGIT_SCALE * d_queries

    def tower_back(inputs_ref, first_ref, second_ref, slot):
        unit = units_ref[slot]
        d_unit = d_units_ref[slot]
        along = jnp.sum(unit * d_unit, axis=1, keepdims=True)
        d_outer = ((d_unit - unit * along) / radii_ref[slot]).astype(BF16)
        inputs = inputs_ref[...]
        h = second_ref.shape[0]
        pre = jnp.dot(inputs, first_ref[...], preferred_element_type=F32)
        sigma = jax.nn.sigmoid(pre)
        hidden = (pre * sigma).astype(BF16)
        grads_ref[slot, h:] = contract_lead(hidden, d_outer)
        d_hidden = contract_last(d_outer, second_ref[...])
        d_pre = (d_hidden * sigma * (1.0 + pre * (1.0 - sigma))).astype(BF16)
        first_grad = contract_lead(inputs, d_pre)
        for j in range(h // LANES):
            grads_ref[slot, j * LANES : (j + 1) * LANES] = first_grad[:, j * LANES : (j + 1) * LANES]
        return d_pre

    tower_back(feats_ref, iw1_ref, iw2_ref, 1)
    d_pre = tower_back(pooled_ref, qw1_ref, qw2_ref, 0)
    d_x_ref[...] = contract_last(d_pre, qw1_ref[...])
    keep_ref[...] = grads_ref[core]
    send_ref[...] = grads_ref[1 - core].astype(BF16)


def rows_kernel(tally_ref, counts_ref, d_x_ref, table_ref, state_ref, new_ref):
    counts = column_of(counts_ref[...].astype(F32))
    pieces = three_pieces(d_x_ref[...] / counts)
    row_grads = add_pieces(jnp.dot(tally_ref[...], pieces, preferred_element_type=F32))
    mean = jnp.mean(row_grads * row_grads, axis=1, keepdims=True)
    acc = column_of(state_ref[...]) + mean
    new_ref[...] = table_ref[...] - LEARNING_RATE * row_grads / jnp.sqrt(acc)


def finish_kernel(mine, where_ref, source_ref, *refs):
    q1_ref, q2_ref, i1_ref, i2_ref, first_ref, second_ref, sent = refs[-7:]
    core = where_ref[1]
    e, h = first_ref.shape

    def copies(first_hbm, second_hbm):
        return [
            pltpu.make_async_copy(first_ref, first_hbm, sent.at[0]),
            pltpu.make_async_copy(second_ref, second_hbm, sent.at[1]),
        ]

    def write(first_hbm, second_hbm):
        first, second = copies(first_hbm, second_hbm)
        second_ref[...] = source_ref[h:].astype(F32)
        second.start()
        for i in range(h // LANES):
            first_ref[:, i * LANES : (i + 1) * LANES] = source_ref[i * LANES : (i + 1) * LANES].astype(F32)
        first.start()
        second.wait()
        first.wait()

    query_tower = (core == 0) if mine else (core != 0)

    @pl.when(query_tower)
    def _():
        write(q1_ref, q2_ref)

    @pl.when(jnp.logical_not(query_tower))
    def _():
        write(i1_ref, i2_ref)


VMEM = pl.BlockSpec(memory_space=pltpu.VMEM)
SMEM = pl.BlockSpec(memory_space=pltpu.SMEM)
HBM = pl.BlockSpec(memory_space=pltpu.HBM)


def call(kernel, out_shape, operands, in_specs=None, out_specs=None, scratch=(), flops=0, limit=32, aliases=None):
    return pl.pallas_call(
        kernel,
        out_shape=out_shape,
        in_specs=in_specs or [VMEM] * len(operands),
        out_specs=out_specs or jax.tree.map(lambda _: VMEM, out_shape),
        scratch_shapes=list(scratch),
        input_output_aliases=aliases or {},
        compiler_params=pltpu.CompilerParams(vmem_limit_bytes=limit * 2**20),
        cost_estimate=pl.CostEstimate(flops=flops, bytes_accessed=2**20, transcendentals=0),
    )(*operands)


def exchange(values, axes):
    return lax.all_to_all(values, axes, 0, 0, tiled=True)


def per_device(rows, state, bag_ids, bag_counts, item_feats, positives, q_w1, q_w2, i_w1, i_w2):
    group = ("y", "xl")
    block = ("y", "xl", "zp", "xh")
    struct = jax.ShapeDtypeStruct
    ranks = lax.axis_size(group)
    spread = lax.axis_size(block)
    table = rows[0]
    feats = item_feats[0]
    q_rows, e = bag_ids.shape[1], table.shape[1]
    i_rows = feats.shape[0]
    h = q_w2.shape[0]
    where = jnp.stack([lax.axis_index(group), lax.axis_index("c")]).astype(jnp.int32)

    ids = bag_ids[0].T
    arguments = [ids, bag_counts, positives, table, feats, q_w1, q_w2, i_w1, i_w2]
    payload, pooled, tally, units, radii = call(
        front_kernel,
        [
            struct((ranks, q_rows + i_rows + CODE_ROWS, e), BF16),
            struct((q_rows, e), BF16),
            struct((table.shape[0], q_rows), BF16),
            struct((2, q_rows, e), F32),
            struct((2, q_rows, e), F32),
        ],
        arguments,
        in_specs=[HBM] * len(arguments),
        scratch=[pltpu.VMEM(a.shape, a.dtype) for a in arguments]
        + [pltpu.SemaphoreType.DMA((len(arguments),))],
        limit=60,
    )
    everyone = exchange(payload, group)
    keep, send, d_x = call(
        middle_kernel,
        [struct((2 * h, e), F32), struct((2 * h, e), BF16), struct((q_rows, e), F32)],
        [where, everyone, positives, pooled, feats, units, radii, q_w1, q_w2, i_w1, i_w2],
        in_specs=[SMEM] + [VMEM] * 10,
        scratch=[
            pltpu.VMEM((ranks, 8, q_rows), F32),
            pltpu.VMEM((ranks, 8, q_rows), jnp.int32),
            pltpu.VMEM((2, q_rows, e), F32),
            pltpu.VMEM((2, 2 * h, e), F32),
        ],
    )
    swap = [(0, 1), (1, 0)]
    received = lax.ppermute(send, "c", swap)
    new_rows = call(
        rows_kernel, struct(table.shape, F32), [tally, bag_counts, d_x, table, state], flops=2**30
    )
    chip_sum = (keep + received.astype(F32)).astype(BF16).reshape(spread, 2 * h // spread, e)
    chip_sum, new_rows = lax.optimization_barrier((chip_sum, new_rows))
    mine = jnp.sum(exchange(chip_sum, block).astype(F32), axis=0).astype(BF16)
    copies = jnp.broadcast_to(mine, (lax.axis_size("zh"),) + mine.shape)
    mine = jnp.sum(exchange(copies, "zh").astype(F32), axis=0).astype(BF16)
    copies = jnp.broadcast_to(mine, (spread,) + mine.shape)
    tower = exchange(copies, block).reshape(2 * h, e)
    other = lax.ppermute(tower, "c", swap)
    shapes = [struct((e, h), F32), struct((h, e), F32), struct((e, h), F32), struct((h, e), F32)]
    buffers = [pltpu.VMEM((e, h), F32), pltpu.VMEM((h, e), F32), pltpu.SemaphoreType.DMA((2,))]
    own = call(
        functools.partial(finish_kernel, True),
        shapes,
        [where, tower],
        in_specs=[SMEM, VMEM],
        out_specs=[HBM] * 4,
        scratch=buffers,
        flops=2**30,
    )
    sums = call(
        functools.partial(finish_kernel, False),
        shapes,
        [where, other, *own],
        in_specs=[SMEM, VMEM] + [HBM] * 4,
        out_specs=[HBM] * 4,
        scratch=buffers,
        aliases={2: 0, 3: 1, 4: 2, 5: 3},
    )
    return (new_rows[None], *sums)


def solution(mesh):
    blk, rep = mesh.devices.shape
    parts = (blk // 2, 2, max(rep // 8, 1), 2 if rep >= 8 else 1, 2 if rep >= 4 else 1, 2)
    fine = Mesh(mesh.devices.reshape(parts), ("y", "xl", "zh", "zp", "xh", "c"))
    rep_axes = ("zh", "zp", "xh", "c")
    blk_axes = ("y", "xl")
    in_specs = (
        P(rep_axes, blk_axes, None),
        P(rep_axes, blk_axes),
        P(rep_axes, blk_axes, None),
        P(rep_axes, blk_axes),
        P(rep_axes, blk_axes, None),
        P(rep_axes, blk_axes),
        P(),
        P(),
        P(),
        P(),
    )
    out_specs = (P(rep_axes, blk_axes, None), P(), P(), P(), P())
    return jax.shard_map(
        per_device, mesh=fine, in_specs=in_specs, out_specs=out_specs, check_vma=False
    )
```

```python
import jax
import jax.numpy as jnp
from jax import lax
from jax.experimental import pallas as pl
from jax.experimental.pallas import tpu as pltpu
from jax.sharding import Mesh, PartitionSpec as P

LOGIT_SCALE = 20.0
EXP_SCALE = 28.853900817779268
LEARNING_RATE = 0.5
NORM_EPS = 1e-06

BF16 = jnp.bfloat16
F32 = jnp.float32

CODE_ROWS = 16
LANES = 128


def contract_lead(left, right):
    return lax.dot_general(left, right, (((0,), (0,)), ((), ())), preferred_element_type=F32)


def contract_last(left, right):
    return lax.dot_general(left, right, (((1,), (1,)), ((), ())), preferred_element_type=F32)


def column_of(row):
    return jnp.transpose(jnp.broadcast_to(row, (LANES, row.shape[1])))


def three_pieces(values):
    high = values.astype(BF16)
    rest = values - high.astype(F32)
    middle = rest.astype(BF16)
    low = (rest - middle.astype(F32)).astype(BF16)
    return jnp.concatenate([high, middle, low], axis=1)


def add_pieces(product):
    return (product[:, 2 * LANES :] + product[:, LANES : 2 * LANES]) + product[:, :LANES]


def radius_of(outer):
    return jnp.sqrt(jnp.sum(outer * outer, axis=1, keepdims=True) + NORM_EPS)


def front_kernel(
    ids_hbm, counts_hbm, pos_hbm, table_hbm, feats_hbm, qw1_hbm, qw2_hbm, iw1_hbm, iw2_hbm,
    payload_ref, pooled_ref, tally_ref, outers_ref,
    ids_ref, counts_ref, pos_ref, table_ref, feats_ref, qw1_ref, qw2_ref, iw1_ref, iw2_ref, arrived,
):
    sources = (ids_hbm, counts_hbm, table_hbm, qw1_hbm, feats_hbm, iw1_hbm, qw2_hbm, iw2_hbm, pos_hbm)
    targets = (ids_ref, counts_ref, table_ref, qw1_ref, feats_ref, iw1_ref, qw2_ref, iw2_ref, pos_ref)
    copies = [
        pltpu.make_async_copy(source, target, arrived.at[i])
        for i, (source, target) in enumerate(zip(sources, targets))
    ]
    for copy in copies:
        copy.start()

    members, q_rows = ids_ref.shape
    table_rows = table_ref.shape[0]
    copies[0].wait()
    copies[1].wait()
    counts = counts_ref[...]
    rows = lax.broadcasted_iota(jnp.int32, (table_rows, q_rows), 0)
    tally = jnp.zeros((table_rows, q_rows), F32)
    for m in range(members):
        live = jnp.where(counts > m, ids_ref[m : m + 1], -1)
        tally = tally + jnp.where(live == rows, 1.0, 0.0)
    tally = tally.astype(BF16)
    tally_ref[...] = tally
    copies[2].wait()
    product = contract_lead(tally, three_pieces(table_ref[...]))
    pooled = (add_pieces(product) / column_of(counts.astype(F32))).astype(BF16)
    pooled_ref[...] = pooled

    def tower(inputs, first, second, slot):
        copies[first].wait()
        pre = jnp.dot(inputs, targets[first][...], preferred_element_type=F32)
        hidden = (pre * jax.nn.sigmoid(pre)).astype(BF16)
        copies[second].wait()
        outer = jnp.dot(hidden, targets[second][...], preferred_element_type=F32)
        outers_ref[slot] = outer
        return (outer / radius_of(outer)).astype(BF16)

    queries = tower(pooled, 3, 6, 0)
    copies[4].wait()
    keys = tower(feats_ref[...], 5, 7, 1)
    copies[8].wait()
    pos = pos_ref[...]
    digits = jnp.concatenate([pos // LANES, pos % LANES], axis=0).astype(F32)
    spread = jnp.concatenate(
        [digits[:, i * LANES : (i + 1) * LANES] for i in range(q_rows // LANES)]
        + [jnp.zeros((CODE_ROWS - 2 * (q_rows // LANES), LANES), F32)],
        axis=0,
    ).astype(BF16)
    for copy in range(payload_ref.shape[0]):
        payload_ref[copy, :q_rows] = queries
        payload_ref[copy, q_rows : 2 * q_rows] = keys
        payload_ref[copy, 2 * q_rows :] = spread


def prepare_kernel(
    where_ref, pooled_ref, feats_ref, other_ref, qw1_ref, qw2_ref, iw1_ref, iw2_ref,
    slope_ref, hidden_ref, inputs_ref, second_ref,
    both_ref, first_ref,
):
    core = where_ref[1]
    rows = other_ref.shape[0]

    @pl.when(core == 0)
    def _():
        both_ref[:rows] = pooled_ref[...]
        first_ref[...] = qw1_ref[...]
        second_ref[...] = qw2_ref[...]

    @pl.when(core != 0)
    def _():
        both_ref[:rows] = feats_ref[...]
        first_ref[...] = iw1_ref[...]
        second_ref[...] = iw2_ref[...]

    both_ref[rows:] = other_ref[...]
    both = both_ref[...]
    inputs_ref[...] = jnp.transpose(both)
    pre = jnp.dot(both, first_ref[...], preferred_element_type=F32)
    sigma = jax.nn.sigmoid(pre)
    hidden_ref[...] = jnp.transpose((pre * sigma).astype(BF16))
    slope_ref[...] = sigma * (1.0 + pre * (1.0 - sigma))


def outer_grad(d_unit, outer):
    radius = radius_of(outer)
    unit = outer / radius
    along = jnp.sum(unit * d_unit, axis=1, keepdims=True)
    return ((d_unit - unit * along) / radius).astype(BF16)


def middle_kernel(
    where_ref, all_ref, pos_ref, outers_ref,
    d_query_outer_ref, keep_ref, send_ref,
    totals_ref, codes_ref,
):
    ranks = all_ref.shape[0]
    q_rows = outers_ref.shape[1]
    i_rows = outers_ref.shape[1]
    blk = where_ref[0]
    core = where_ref[1]
    norm_c = 1.0 / (q_rows * ranks)

    def add_group(s, carry):
        queries = all_ref[s, :q_rows]

        def add_items(t, partial):
            scores = EXP_SCALE * contract_last(all_ref[t, q_rows : q_rows + i_rows], queries)
            return partial + jnp.sum(jnp.exp2(scores).reshape(i_rows // 8, 8, q_rows), axis=0)

        partial = lax.fori_loop(0, ranks, add_items, jnp.zeros((8, q_rows), F32), unroll=True)
        totals_ref[s] = jnp.broadcast_to(jnp.sum(partial, axis=0, keepdims=True), (8, q_rows))
        digits = all_ref[s, q_rows + i_rows :].astype(F32)
        chunks = q_rows // LANES
        code = jnp.concatenate(
            [digits[2 * i : 2 * i + 1] * LANES + digits[2 * i + 1 : 2 * i + 2] for i in range(chunks)],
            axis=1,
        )
        codes_ref[s] = jnp.broadcast_to(code.astype(jnp.int32), (8, q_rows))
        return carry

    lax.fori_loop(0, ranks, add_group, 0, unroll=True)

    own_keys = all_ref[blk, q_rows : q_rows + i_rows]

    def add_queries(s, d_keys):
        queries = all_ref[s, :q_rows]
        shares = jnp.exp2(EXP_SCALE * contract_last(own_keys, queries)) * (norm_c / totals_ref[s, :1])
        item = blk * i_rows + lax.broadcasted_iota(jnp.int32, (i_rows, q_rows), 0)
        weights = (shares - jnp.where(codes_ref[s, :1] == item, norm_c, 0.0)).astype(BF16)
        return d_keys + jnp.dot(weights, queries, preferred_element_type=F32)


    own_queries = all_ref[blk, :q_rows]
    inverse = column_of(norm_c / totals_ref[blk, :1])
    inverse = jnp.concatenate([inverse] * (i_rows // LANES), axis=1)
    target = jnp.concatenate([column_of(pos_ref[...])] * (i_rows // LANES), axis=1)
    target = target - lax.broadcasted_iota(jnp.int32, (q_rows, i_rows), 1)

    def add_keys(t, d_queries):
        keys = all_ref[t, q_rows : q_rows + i_rows]
        shares = jnp.exp2(EXP_SCALE * contract_last(own_queries, keys)) * inverse
        weights = (shares - jnp.where(target == t * i_rows, norm_c, 0.0)).astype(BF16)
        return d_queries + jnp.dot(weights, keys, preferred_element_type=F32)

    d_keys = jnp.zeros((i_rows, LANES), F32)
    d_queries = jnp.zeros((q_rows, LANES), F32)
    for r in range(ranks):
        d_keys = add_queries(r, d_keys)
        d_queries = add_keys(r, d_queries)

    d_key_outer = outer_grad(LOGIT_SCALE * d_keys, outers_ref[1])
    d_query_outer = outer_grad(LOGIT_SCALE * d_queries, outers_ref[0])
    d_query_outer_ref[...] = d_query_outer

    @pl.when(core == 0)
    def _():
        keep_ref[...] = d_query_outer
        send_ref[...] = d_key_outer

    @pl.when(core != 0)
    def _():
        keep_ref[...] = d_key_outer
        send_ref[...] = d_query_outer


def back_kernel(keep_ref, received_ref, slope_ref, hidden_ref, inputs_ref, second_ref, grads_ref):
    h = second_ref.shape[0]
    d_outer = jnp.concatenate([keep_ref[...], received_ref[...]], axis=0)
    grads_ref[h:] = jnp.dot(hidden_ref[...], d_outer, preferred_element_type=F32).astype(BF16)
    d_pre = (contract_last(d_outer, second_ref[...]) * slope_ref[...]).astype(BF16)
    first_grad = jnp.dot(inputs_ref[...], d_pre, preferred_element_type=F32).astype(BF16)
    for j in range(h // LANES):
        grads_ref[j * LANES : (j + 1) * LANES] = first_grad[:, j * LANES : (j + 1) * LANES]


def rows_kernel(
    tally_ref, counts_ref, pooled_ref, d_outer_ref, qw1_ref, qw2_ref, table_ref, state_ref, new_ref
):
    pre = jnp.dot(pooled_ref[...], qw1_ref[...], preferred_element_type=F32)
    sigma = jax.nn.sigmoid(pre)
    d_hidden = contract_last(d_outer_ref[...], qw2_ref[...])
    d_pre = (d_hidden * (sigma * (1.0 + pre * (1.0 - sigma)))).astype(BF16)
    d_x = contract_last(d_pre, qw1_ref[...])
    counts = column_of(counts_ref[...].astype(F32))
    pieces = three_pieces(d_x / counts)
    row_grads = add_pieces(jnp.dot(tally_ref[...], pieces, preferred_element_type=F32))
    mean = jnp.mean(row_grads * row_grads, axis=1, keepdims=True)
    acc = column_of(state_ref[...]) + mean
    new_ref[...] = table_ref[...] - LEARNING_RATE * row_grads / jnp.sqrt(acc)


def finish_kernel(
    where_ref, mine_ref, other_ref, q1_ref, q2_ref, i1_ref, i2_ref, first_ref, second_ref, sent
):
    core = where_ref[1]
    h = second_ref.shape[1]

    def write(query_source, item_source):
        copies = []
        for slot, (source_ref, first_hbm, second_hbm) in enumerate(
            ((query_source, q1_ref, q2_ref), (item_source, i1_ref, i2_ref))
        ):
            second_ref[slot] = source_ref[h:].astype(F32)
            copies.append(pltpu.make_async_copy(second_ref.at[slot], second_hbm, sent.at[slot, 0]))
            copies[-1].start()
            for j in range(0, h, LANES):
                first_ref[slot, :, j : j + LANES] = source_ref[j : j + LANES].astype(F32)
            copies.append(pltpu.make_async_copy(first_ref.at[slot], first_hbm, sent.at[slot, 1]))
            copies[-1].start()
        for copy in copies:
            copy.wait()

    @pl.when(core == 0)
    def _():
        write(mine_ref, other_ref)

    @pl.when(core != 0)
    def _():
        write(other_ref, mine_ref)


VMEM = pl.BlockSpec(memory_space=pltpu.VMEM)
SMEM = pl.BlockSpec(memory_space=pltpu.SMEM)
HBM = pl.BlockSpec(memory_space=pltpu.HBM)


def call(kernel, out_shape, operands, in_specs=None, out_specs=None, scratch=(), flops=0, limit=32):
    return pl.pallas_call(
        kernel,
        out_shape=out_shape,
        in_specs=in_specs or [VMEM] * len(operands),
        out_specs=out_specs or jax.tree.map(lambda _: VMEM, out_shape),
        scratch_shapes=list(scratch),
        compiler_params=pltpu.CompilerParams(vmem_limit_bytes=limit * 2**20),
        cost_estimate=pl.CostEstimate(flops=flops, bytes_accessed=2**20, transcendentals=0),
    )(*operands)


def exchange(values, axes):
    return lax.all_to_all(values, axes, 0, 0, tiled=True)


def per_device(rows, state, bag_ids, bag_counts, item_feats, positives, q_w1, q_w2, i_w1, i_w2):
    group = ("y", "xl")
    block = ("y", "xl", "zp", "xh")
    struct = jax.ShapeDtypeStruct
    ranks = lax.axis_size(group)
    spread = lax.axis_size(block)
    table = rows[0]
    feats = item_feats[0]
    q_rows, e = bag_ids.shape[1], table.shape[1]
    i_rows = feats.shape[0]
    h = q_w2.shape[0]
    where = jnp.stack([lax.axis_index(group), lax.axis_index("c")]).astype(jnp.int32)

    ids = bag_ids[0].T
    arguments = [ids, bag_counts, positives, table, feats, q_w1, q_w2, i_w1, i_w2]
    payload, pooled, tally, outers = call(
        front_kernel,
        [
            struct((ranks, q_rows + i_rows + CODE_ROWS, e), BF16),
            struct((q_rows, e), BF16),
            struct((table.shape[0], q_rows), BF16),
            struct((2, q_rows, e), F32),
        ],
        arguments,
        in_specs=[HBM] * len(arguments),
        scratch=[pltpu.VMEM(a.shape, a.dtype) for a in arguments]
        + [pltpu.SemaphoreType.DMA((len(arguments),))],
        limit=60,
    )
    everyone = exchange(payload, group)
    swap = [(0, 1), (1, 0)]
    other_inputs = lax.ppermute(jnp.where(where[1] == 0, feats, pooled), "c", swap)
    prepared = call(
        prepare_kernel,
        [
            struct((2 * q_rows, h), F32),
            struct((h, 2 * q_rows), BF16),
            struct((e, 2 * q_rows), BF16),
            struct((h, e), BF16),
        ],
        [where, pooled, feats, other_inputs, q_w1, q_w2, i_w1, i_w2],
        in_specs=[SMEM] + [VMEM] * 7,
        scratch=[pltpu.VMEM((2 * q_rows, e), BF16), pltpu.VMEM((e, h), BF16)],
        flops=2**28,
    )
    d_query_outer, keep, send = call(
        middle_kernel,
        [struct((q_rows, e), BF16)] * 3,
        [where, everyone, positives, outers],
        in_specs=[SMEM] + [VMEM] * 3,
        scratch=[pltpu.VMEM((ranks, 8, q_rows), F32), pltpu.VMEM((ranks, 8, q_rows), jnp.int32)],
    )
    received = lax.ppermute(send, "c", swap)
    grads = call(back_kernel, struct((2 * h, e), BF16), [keep, received, *prepared])
    new_rows = call(
        rows_kernel,
        struct(table.shape, F32),
        [tally, bag_counts, pooled, d_query_outer, q_w1, q_w2, table, state],
        flops=2**30,
    )
    chip_sum = grads.reshape(spread, 2 * h // spread, e)
    mine = jnp.sum(exchange(chip_sum, block).astype(F32), axis=0).astype(BF16)
    copies = jnp.broadcast_to(mine, (lax.axis_size("zh"),) + mine.shape)
    mine = jnp.sum(exchange(copies, "zh").astype(F32), axis=0).astype(BF16)
    copies = jnp.broadcast_to(mine, (spread,) + mine.shape)
    tower = exchange(copies, block).reshape(2 * h, e)
    other = lax.ppermute(tower, "c", swap)
    sums = call(
        finish_kernel,
        [struct((e, h), F32), struct((h, e), F32), struct((e, h), F32), struct((h, e), F32)],
        [where, tower, other],
        in_specs=[SMEM, VMEM, VMEM],
        out_specs=[HBM] * 4,
        scratch=[
            pltpu.VMEM((2, e, h), F32),
            pltpu.VMEM((2, h, e), F32),
            pltpu.SemaphoreType.DMA((2, 2)),
        ],
    )
    return (new_rows[None], *sums)


def solution(mesh):
    blk, rep = mesh.devices.shape
    parts = (blk // 2, 2, max(rep // 8, 1), 2 if rep >= 8 else 1, 2 if rep >= 4 else 1, 2)
    fine = Mesh(mesh.devices.reshape(parts), ("y", "xl", "zh", "zp", "xh", "c"))
    rep_axes = ("zh", "zp", "xh", "c")
    blk_axes = ("y", "xl")
    in_specs = (
        P(rep_axes, blk_axes, None),
        P(rep_axes, blk_axes),
        P(rep_axes, blk_axes, None),
        P(rep_axes, blk_axes),
        P(rep_axes, blk_axes, None),
        P(rep_axes, blk_axes),
        P(),
        P(),
        P(),
        P(),
    )
    out_specs = (P(rep_axes, blk_axes, None), P(), P(), P(), P())
    return jax.shard_map(
        per_device, mesh=fine, in_specs=in_specs, out_specs=out_specs, check_vma=False
    )
```

```python
import jax
import jax.numpy as jnp
from jax import lax
from jax.experimental import pallas as pl
from jax.experimental.pallas import tpu as pltpu
from jax.sharding import Mesh, PartitionSpec as P

LOGIT_SCALE = 20.0
EXP_SCALE = 28.853900817779268
LEARNING_RATE = 0.5
NORM_EPS = 1e-06

BF16 = jnp.bfloat16
F32 = jnp.float32

CODE_ROWS = 16
LANES = 128


def contract_lead(left, right):
    return lax.dot_general(left, right, (((0,), (0,)), ((), ())), preferred_element_type=F32)


def contract_last(left, right):
    return lax.dot_general(left, right, (((1,), (1,)), ((), ())), preferred_element_type=F32)


def column_of(row):
    return jnp.transpose(jnp.broadcast_to(row, (LANES, row.shape[1])))


def three_pieces(values):
    high = values.astype(BF16)
    rest = values - high.astype(F32)
    middle = rest.astype(BF16)
    low = (rest - middle.astype(F32)).astype(BF16)
    return jnp.concatenate([high, middle, low], axis=1)


def add_pieces(product):
    return (product[:, 2 * LANES :] + product[:, LANES : 2 * LANES]) + product[:, :LANES]


def radius_of(outer):
    return jnp.sqrt(jnp.sum(outer * outer, axis=1, keepdims=True) + NORM_EPS)


def front_kernel(
    ids_hbm, counts_hbm, pos_hbm, table_hbm, feats_hbm, qw1_hbm, qw2_hbm, iw1_hbm, iw2_hbm,
    payload_ref, pooled_ref, tally_ref, outers_ref,
    ids_ref, counts_ref, pos_ref, table_ref, feats_ref, qw1_ref, qw2_ref, iw1_ref, iw2_ref, arrived,
):
    sources = (ids_hbm, counts_hbm, table_hbm, qw1_hbm, feats_hbm, iw1_hbm, qw2_hbm, iw2_hbm, pos_hbm)
    targets = (ids_ref, counts_ref, table_ref, qw1_ref, feats_ref, iw1_ref, qw2_ref, iw2_ref, pos_ref)
    copies = [
        pltpu.make_async_copy(source, target, arrived.at[i])
        for i, (source, target) in enumerate(zip(sources, targets))
    ]
    for copy in copies:
        copy.start()

    members, q_rows = ids_ref.shape
    table_rows = table_ref.shape[0]
    copies[0].wait()
    copies[1].wait()
    counts = counts_ref[...]
    rows = lax.broadcasted_iota(jnp.int32, (table_rows, q_rows), 0)
    tally = jnp.zeros((table_rows, q_rows), F32)
    for m in range(members):
        live = jnp.where(counts > m, ids_ref[m : m + 1], -1)
        tally = tally + jnp.where(live == rows, 1.0, 0.0)
    tally = tally.astype(BF16)
    tally_ref[...] = tally
    copies[2].wait()
    product = contract_lead(tally, three_pieces(table_ref[...]))
    pooled = (add_pieces(product) / column_of(counts.astype(F32))).astype(BF16)
    pooled_ref[...] = pooled

    def tower(inputs, first, second, slot):
        copies[first].wait()
        pre = jnp.dot(inputs, targets[first][...], preferred_element_type=F32)
        hidden = (pre * jax.nn.sigmoid(pre)).astype(BF16)
        copies[second].wait()
        outer = jnp.dot(hidden, targets[second][...], preferred_element_type=F32)
        outers_ref[slot] = outer
        return (outer / radius_of(outer)).astype(BF16)

    queries = tower(pooled, 3, 6, 0)
    copies[4].wait()
    keys = tower(feats_ref[...], 5, 7, 1)
    copies[8].wait()
    pos = pos_ref[...]
    digits = jnp.concatenate([pos // LANES, pos % LANES], axis=0).astype(F32)
    spread = jnp.concatenate(
        [digits[:, i * LANES : (i + 1) * LANES] for i in range(q_rows // LANES)]
        + [jnp.zeros((CODE_ROWS - 2 * (q_rows // LANES), LANES), F32)],
        axis=0,
    ).astype(BF16)
    for copy in range(payload_ref.shape[0]):
        payload_ref[copy, :q_rows] = queries
        payload_ref[copy, q_rows : 2 * q_rows] = keys
        payload_ref[copy, 2 * q_rows :] = spread


def backward(inputs, hidden_t, slope, d_outer, second):
    d_pre = (contract_last(d_outer, second) * slope).astype(BF16)
    return contract_lead(inputs, d_pre), jnp.dot(hidden_t, d_outer, preferred_element_type=F32)


def forward(inputs, first):
    pre = jnp.dot(inputs, first, preferred_element_type=F32)
    sigma = jax.nn.sigmoid(pre)
    return jnp.transpose((pre * sigma).astype(BF16)), sigma * (1.0 + pre * (1.0 - sigma))


def prepare_kernel(
    where_ref, keep_ref, qw1_ref, qw2_ref, iw1_ref, iw2_ref,
    hidden_ref, slope_ref, first_ref, second_ref,
):
    core = where_ref[1]

    @pl.when(core == 0)
    def _():
        first_ref[...] = qw1_ref[...]
        second_ref[...] = qw2_ref[...]

    @pl.when(core != 0)
    def _():
        first_ref[...] = iw1_ref[...]
        second_ref[...] = iw2_ref[...]

    hidden_ref[...], slope_ref[...] = forward(keep_ref[keep_ref.shape[0] // 2 :], first_ref[...])


def outer_grad(d_unit, outer):
    radius = radius_of(outer)
    unit = outer / radius
    along = jnp.sum(unit * d_unit, axis=1, keepdims=True)
    return ((d_unit - unit * along) / radius).astype(BF16)


def middle_kernel(
    where_ref, all_ref, pos_ref, outers_ref, pooled_ref, feats_ref,
    d_query_outer_ref, keep_ref, send_ref,
    totals_ref, codes_ref,
):
    ranks = all_ref.shape[0]
    q_rows = outers_ref.shape[1]
    i_rows = outers_ref.shape[1]
    blk = where_ref[0]
    core = where_ref[1]
    norm_c = 1.0 / (q_rows * ranks)

    def add_group(s, carry):
        queries = all_ref[s, :q_rows]

        def add_items(t, partial):
            scores = EXP_SCALE * contract_last(all_ref[t, q_rows : q_rows + i_rows], queries)
            return partial + jnp.sum(jnp.exp2(scores).reshape(i_rows // 8, 8, q_rows), axis=0)

        partial = lax.fori_loop(0, ranks, add_items, jnp.zeros((8, q_rows), F32), unroll=True)
        totals_ref[s] = jnp.broadcast_to(jnp.sum(partial, axis=0, keepdims=True), (8, q_rows))
        digits = all_ref[s, q_rows + i_rows :].astype(F32)
        chunks = q_rows // LANES
        code = jnp.concatenate(
            [digits[2 * i : 2 * i + 1] * LANES + digits[2 * i + 1 : 2 * i + 2] for i in range(chunks)],
            axis=1,
        )
        codes_ref[s] = jnp.broadcast_to(code.astype(jnp.int32), (8, q_rows))
        return carry

    lax.fori_loop(0, ranks, add_group, 0, unroll=True)

    own_keys = all_ref[blk, q_rows : q_rows + i_rows]

    def add_queries(s, d_keys):
        queries = all_ref[s, :q_rows]
        shares = jnp.exp2(EXP_SCALE * contract_last(own_keys, queries)) * (norm_c / totals_ref[s, :1])
        item = blk * i_rows + lax.broadcasted_iota(jnp.int32, (i_rows, q_rows), 0)
        weights = (shares - jnp.where(codes_ref[s, :1] == item, norm_c, 0.0)).astype(BF16)
        return d_keys + jnp.dot(weights, queries, preferred_element_type=F32)


    own_queries = all_ref[blk, :q_rows]
    inverse = column_of(norm_c / totals_ref[blk, :1])
    inverse = jnp.concatenate([inverse] * (i_rows // LANES), axis=1)
    target = jnp.concatenate([column_of(pos_ref[...])] * (i_rows // LANES), axis=1)
    target = target - lax.broadcasted_iota(jnp.int32, (q_rows, i_rows), 1)

    def add_keys(t, d_queries):
        keys = all_ref[t, q_rows : q_rows + i_rows]
        shares = jnp.exp2(EXP_SCALE * contract_last(own_queries, keys)) * inverse
        weights = (shares - jnp.where(target == t * i_rows, norm_c, 0.0)).astype(BF16)
        return d_queries + jnp.dot(weights, keys, preferred_element_type=F32)

    d_keys = jnp.zeros((i_rows, LANES), F32)
    d_queries = jnp.zeros((q_rows, LANES), F32)
    for r in range(ranks):
        d_keys = add_queries(r, d_keys)
        d_queries = add_keys(r, d_queries)

    d_key_outer = outer_grad(LOGIT_SCALE * d_keys, outers_ref[1])
    d_query_outer = outer_grad(LOGIT_SCALE * d_queries, outers_ref[0])
    d_query_outer_ref[...] = d_query_outer

    def split(query_ref, key_ref):
        query_ref[:q_rows] = d_query_outer
        query_ref[q_rows:] = pooled_ref[...]
        key_ref[:i_rows] = d_key_outer
        key_ref[i_rows:] = feats_ref[...]

    @pl.when(core == 0)
    def _():
        split(keep_ref, send_ref)

    @pl.when(core != 0)
    def _():
        split(send_ref, keep_ref)


def back_kernel(keep_ref, received_ref, hidden_ref, slope_ref, first_ref, second_ref, grads_ref):
    h = second_ref.shape[0]
    rows = keep_ref.shape[0] // 2
    second = second_ref[...]
    hidden_t, slope = forward(received_ref[rows:], first_ref[...])
    first_mine, second_mine = backward(keep_ref[rows:], hidden_ref[...], slope_ref[...], keep_ref[:rows], second)
    first_other, second_other = backward(received_ref[rows:], hidden_t, slope, received_ref[:rows], second)
    grads_ref[h:] = (second_mine + second_other).astype(BF16)
    first_grad = (first_mine + first_other).astype(BF16)
    for j in range(h // LANES):
        grads_ref[j * LANES : (j + 1) * LANES] = first_grad[:, j * LANES : (j + 1) * LANES]


def rows_kernel(
    tally_ref, counts_ref, pooled_ref, d_outer_ref, qw1_ref, qw2_ref, table_ref, state_ref, new_ref
):
    pre = jnp.dot(pooled_ref[...], qw1_ref[...], preferred_element_type=F32)
    sigma = jax.nn.sigmoid(pre)
    d_hidden = contract_last(d_outer_ref[...], qw2_ref[...])
    d_pre = (d_hidden * (sigma * (1.0 + pre * (1.0 - sigma)))).astype(BF16)
    d_x = contract_last(d_pre, qw1_ref[...])
    counts = column_of(counts_ref[...].astype(F32))
    pieces = three_pieces(d_x / counts)
    row_grads = add_pieces(jnp.dot(tally_ref[...], pieces, preferred_element_type=F32))
    mean = jnp.mean(row_grads * row_grads, axis=1, keepdims=True)
    acc = column_of(state_ref[...]) + mean
    new_ref[...] = table_ref[...] - LEARNING_RATE * row_grads / jnp.sqrt(acc)


def finish_kernel(
    where_ref, mine_ref, other_ref, q1_ref, q2_ref, i1_ref, i2_ref, first_ref, second_ref, sent
):
    core = where_ref[1]
    h = second_ref.shape[1]

    def write(query_source, item_source):
        copies = []
        for slot, (source_ref, first_hbm, second_hbm) in enumerate(
            ((query_source, q1_ref, q2_ref), (item_source, i1_ref, i2_ref))
        ):
            second_ref[slot] = source_ref[h:].astype(F32)
            copies.append(pltpu.make_async_copy(second_ref.at[slot], second_hbm, sent.at[slot, 0]))
            copies[-1].start()
            for j in range(0, h, LANES):
                first_ref[slot, :, j : j + LANES] = source_ref[j : j + LANES].astype(F32)
            copies.append(pltpu.make_async_copy(first_ref.at[slot], first_hbm, sent.at[slot, 1]))
            copies[-1].start()
        for copy in copies:
            copy.wait()

    @pl.when(core == 0)
    def _():
        write(mine_ref, other_ref)

    @pl.when(core != 0)
    def _():
        write(other_ref, mine_ref)


VMEM = pl.BlockSpec(memory_space=pltpu.VMEM)
SMEM = pl.BlockSpec(memory_space=pltpu.SMEM)
HBM = pl.BlockSpec(memory_space=pltpu.HBM)


def call(kernel, out_shape, operands, in_specs=None, out_specs=None, scratch=(), flops=0, limit=32):
    return pl.pallas_call(
        kernel,
        out_shape=out_shape,
        in_specs=in_specs or [VMEM] * len(operands),
        out_specs=out_specs or jax.tree.map(lambda _: VMEM, out_shape),
        scratch_shapes=list(scratch),
        compiler_params=pltpu.CompilerParams(vmem_limit_bytes=limit * 2**20),
        cost_estimate=pl.CostEstimate(flops=flops, bytes_accessed=2**20, transcendentals=0),
    )(*operands)


def exchange(values, axes):
    return lax.all_to_all(values, axes, 0, 0, tiled=True)


def per_device(rows, state, bag_ids, bag_counts, item_feats, positives, q_w1, q_w2, i_w1, i_w2):
    group = ("y", "xl")
    block = ("y", "xl", "zp", "xh")
    struct = jax.ShapeDtypeStruct
    ranks = lax.axis_size(group)
    spread = lax.axis_size(block)
    table = rows[0]
    feats = item_feats[0]
    q_rows, e = bag_ids.shape[1], table.shape[1]
    i_rows = feats.shape[0]
    h = q_w2.shape[0]
    where = jnp.stack([lax.axis_index(group), lax.axis_index("c")]).astype(jnp.int32)

    ids = bag_ids[0].T
    arguments = [ids, bag_counts, positives, table, feats, q_w1, q_w2, i_w1, i_w2]
    arguments = [pltpu.with_memory_space_constraint(a, pltpu.HBM) for a in arguments]
    payload, pooled, tally, outers = call(
        front_kernel,
        [
            struct((ranks, q_rows + i_rows + CODE_ROWS, e), BF16),
            struct((q_rows, e), BF16),
            struct((table.shape[0], q_rows), BF16),
            struct((2, q_rows, e), F32),
        ],
        arguments,
        in_specs=[HBM] * len(arguments),
        scratch=[pltpu.VMEM(a.shape, a.dtype) for a in arguments]
        + [pltpu.SemaphoreType.DMA((len(arguments),))],
    )
    payload, where = lax.optimization_barrier((payload, where))
    everyone = exchange(payload, group)
    d_query_outer, keep, send = call(
        middle_kernel,
        [struct((q_rows, e), BF16), struct((2 * q_rows, e), BF16), struct((2 * q_rows, e), BF16)],
        [where, everyone, positives, outers, pooled, feats],
        in_specs=[SMEM] + [VMEM] * 5,
        scratch=[pltpu.VMEM((ranks, 8, q_rows), F32), pltpu.VMEM((ranks, 8, q_rows), jnp.int32)],
    )
    swap = [(0, 1), (1, 0)]
    received = lax.ppermute(send, "c", swap)
    prepared = call(
        prepare_kernel,
        [struct((h, q_rows), BF16), struct((q_rows, h), F32), struct((e, h), BF16), struct((h, e), BF16)],
        [where, keep, q_w1, q_w2, i_w1, i_w2],
        in_specs=[SMEM] + [VMEM] * 5,
        flops=2**28,
    )
    grads = call(back_kernel, struct((2 * h, e), BF16), [keep, received, *prepared])
    new_rows = call(
        rows_kernel,
        struct(table.shape, F32),
        [tally, bag_counts, pooled, d_query_outer, q_w1, q_w2, table, state],
        flops=2**30,
    )
    chip_sum = grads.reshape(spread, 2 * h // spread, e)
    mine = jnp.sum(exchange(chip_sum, block).astype(F32), axis=0).astype(BF16)
    copies = jnp.broadcast_to(mine, (lax.axis_size("zh"),) + mine.shape)
    mine = jnp.sum(exchange(copies, "zh").astype(F32), axis=0).astype(BF16)
    copies = jnp.broadcast_to(mine, (spread,) + mine.shape)
    tower = exchange(copies, block).reshape(2 * h, e)
    other = lax.ppermute(tower, "c", swap)
    sums = call(
        finish_kernel,
        [struct((e, h), F32), struct((h, e), F32), struct((e, h), F32), struct((h, e), F32)],
        [where, tower, other],
        in_specs=[SMEM, VMEM, VMEM],
        out_specs=[HBM] * 4,
        scratch=[
            pltpu.VMEM((2, e, h), F32),
            pltpu.VMEM((2, h, e), F32),
            pltpu.SemaphoreType.DMA((2, 2)),
        ],
    )
    return (new_rows[None], *sums)


def solution(mesh):
    blk, rep = mesh.devices.shape
    parts = (blk // 2, 2, max(rep // 8, 1), 2 if rep >= 8 else 1, 2 if rep >= 4 else 1, 2)
    fine = Mesh(mesh.devices.reshape(parts), ("y", "xl", "zh", "zp", "xh", "c"))
    rep_axes = ("zh", "zp", "xh", "c")
    blk_axes = ("y", "xl")
    in_specs = (
        P(rep_axes, blk_axes, None),
        P(rep_axes, blk_axes),
        P(rep_axes, blk_axes, None),
        P(rep_axes, blk_axes),
        P(rep_axes, blk_axes, None),
        P(rep_axes, blk_axes),
        P(),
        P(),
        P(),
        P(),
    )
    out_specs = (P(rep_axes, blk_axes, None), P(), P(), P(), P())
    return jax.shard_map(
        per_device, mesh=fine, in_specs=in_specs, out_specs=out_specs, check_vma=False
    )
```

```python
import functools

import jax
import jax.numpy as jnp
import numpy as np
from jax import lax
from jax.experimental import pallas as pl
from jax.experimental.pallas import tpu as pltpu
from jax.sharding import Mesh, PartitionSpec as P

LOGIT_SCALE = 20.0
EXP_SCALE = 28.853900817779268
LEARNING_RATE = 0.5
NORM_EPS = 1e-06

BF16 = jnp.bfloat16
F32 = jnp.float32

CODE_ROWS = 16
LANES = 128


def contract_lead(left, right):
    return lax.dot_general(left, right, (((0,), (0,)), ((), ())), preferred_element_type=F32)


def contract_last(left, right):
    return lax.dot_general(left, right, (((1,), (1,)), ((), ())), preferred_element_type=F32)


def column_of(row):
    return jnp.transpose(jnp.broadcast_to(row, (LANES, row.shape[1])))


def three_pieces(values):
    high = values.astype(BF16)
    rest = values - high.astype(F32)
    middle = rest.astype(BF16)
    low = (rest - middle.astype(F32)).astype(BF16)
    return jnp.concatenate([high, middle, low], axis=1)


def add_pieces(product):
    return (product[:, 2 * LANES :] + product[:, LANES : 2 * LANES]) + product[:, :LANES]


def radius_of(outer):
    return jnp.sqrt(jnp.sum(outer * outer, axis=1, keepdims=True) + NORM_EPS)


def front_kernel(
    ids_hbm, counts_hbm, pos_hbm, table_hbm, feats_hbm, qw1_hbm, qw2_hbm, iw1_hbm, iw2_hbm,
    payload_ref, pooled_ref, tally_ref, outers_ref,
    ids_ref, counts_ref, pos_ref, table_ref, feats_ref, qw1_ref, qw2_ref, iw1_ref, iw2_ref, arrived,
):
    sources = (ids_hbm, counts_hbm, table_hbm, qw1_hbm, feats_hbm, iw1_hbm, qw2_hbm, iw2_hbm, pos_hbm)
    targets = (ids_ref, counts_ref, table_ref, qw1_ref, feats_ref, iw1_ref, qw2_ref, iw2_ref, pos_ref)
    copies = [
        pltpu.make_async_copy(source, target, arrived.at[i])
        for i, (source, target) in enumerate(zip(sources, targets))
    ]
    for copy in copies:
        copy.start()

    members, q_rows = ids_ref.shape
    table_rows = table_ref.shape[0]
    copies[0].wait()
    copies[1].wait()
    counts = counts_ref[...]
    rows = lax.broadcasted_iota(jnp.int32, (table_rows, q_rows), 0)
    tally = jnp.zeros((table_rows, q_rows), F32)
    for m in range(members):
        live = jnp.where(counts > m, ids_ref[m : m + 1], -1)
        tally = tally + jnp.where(live == rows, 1.0, 0.0)
    tally = tally.astype(BF16)
    tally_ref[...] = tally
    copies[2].wait()
    product = contract_lead(tally, three_pieces(table_ref[...]))
    pooled = (add_pieces(product) / column_of(counts.astype(F32))).astype(BF16)
    pooled_ref[...] = pooled

    def tower(inputs, first, second, slot):
        copies[first].wait()
        pre = jnp.dot(inputs, targets[first][...], preferred_element_type=F32)
        hidden = (pre * jax.nn.sigmoid(pre)).astype(BF16)
        copies[second].wait()
        outer = jnp.dot(hidden, targets[second][...], preferred_element_type=F32)
        outers_ref[slot] = outer
        return (outer / radius_of(outer)).astype(BF16)

    queries = tower(pooled, 3, 6, 0)
    copies[4].wait()
    keys = tower(feats_ref[...], 5, 7, 1)
    copies[8].wait()
    pos = pos_ref[...]
    digits = jnp.concatenate([pos // LANES, pos % LANES], axis=0).astype(F32)
    spread = jnp.concatenate(
        [digits[:, i * LANES : (i + 1) * LANES] for i in range(q_rows // LANES)]
        + [jnp.zeros((CODE_ROWS - 2 * (q_rows // LANES), LANES), F32)],
        axis=0,
    ).astype(BF16)
    for copy in range(payload_ref.shape[0]):
        payload_ref[copy, :q_rows] = queries
        payload_ref[copy, q_rows : 2 * q_rows] = keys
        payload_ref[copy, 2 * q_rows :] = spread


def backward(inputs, hidden_t, slope, d_outer, second):
    d_pre = (contract_last(d_outer, second) * slope).astype(BF16)
    return contract_lead(inputs, d_pre), jnp.dot(hidden_t, d_outer, preferred_element_type=F32)


def forward(inputs, first):
    pre = jnp.dot(inputs, first, preferred_element_type=F32)
    sigma = jax.nn.sigmoid(pre)
    return jnp.transpose((pre * sigma).astype(BF16)), sigma * (1.0 + pre * (1.0 - sigma))


def prepare_kernel(
    where_ref, keep_ref, qw1_ref, qw2_ref, iw1_ref, iw2_ref,
    hidden_ref, slope_ref, first_ref, second_ref,
):
    core = where_ref[1]

    @pl.when(core == 0)
    def _():
        first_ref[...] = qw1_ref[...]
        second_ref[...] = qw2_ref[...]

    @pl.when(core != 0)
    def _():
        first_ref[...] = iw1_ref[...]
        second_ref[...] = iw2_ref[...]

    hidden_ref[...], slope_ref[...] = forward(keep_ref[keep_ref.shape[0] // 2 :], first_ref[...])


def outer_grad(d_unit, outer):
    radius = radius_of(outer)
    unit = outer / radius
    along = jnp.sum(unit * d_unit, axis=1, keepdims=True)
    return ((d_unit - unit * along) / radius).astype(BF16)


def middle_kernel(
    order, where_ref, all_ref, pos_ref, outers_ref, pooled_ref, feats_ref,
    d_query_outer_ref, keep_ref, send_ref,
    totals_ref, codes_ref,
):
    ranks = all_ref.shape[0]
    q_rows = outers_ref.shape[1]
    i_rows = outers_ref.shape[1]
    slot = where_ref[0]
    core = where_ref[1]
    item_start = where_ref[2] * i_rows
    norm_c = 1.0 / (q_rows * ranks)

    def add_group(s, carry):
        queries = all_ref[s, :q_rows]

        def add_items(t, partial):
            scores = EXP_SCALE * contract_last(all_ref[t, q_rows : q_rows + i_rows], queries)
            return partial + jnp.sum(jnp.exp2(scores).reshape(i_rows // 8, 8, q_rows), axis=0)

        partial = lax.fori_loop(0, ranks, add_items, jnp.zeros((8, q_rows), F32), unroll=True)
        totals_ref[s] = jnp.broadcast_to(jnp.sum(partial, axis=0, keepdims=True), (8, q_rows))
        digits = all_ref[s, q_rows + i_rows :].astype(F32)
        chunks = q_rows // LANES
        code = jnp.concatenate(
            [digits[2 * i : 2 * i + 1] * LANES + digits[2 * i + 1 : 2 * i + 2] for i in range(chunks)],
            axis=1,
        )
        codes_ref[s] = jnp.broadcast_to(code.astype(jnp.int32), (8, q_rows))
        return carry

    lax.fori_loop(0, ranks, add_group, 0, unroll=True)

    own_keys = all_ref[slot, q_rows : q_rows + i_rows]

    def add_queries(s, d_keys):
        queries = all_ref[s, :q_rows]
        shares = jnp.exp2(EXP_SCALE * contract_last(own_keys, queries)) * (norm_c / totals_ref[s, :1])
        item = item_start + lax.broadcasted_iota(jnp.int32, (i_rows, q_rows), 0)
        weights = (shares - jnp.where(codes_ref[s, :1] == item, norm_c, 0.0)).astype(BF16)
        return d_keys + jnp.dot(weights, queries, preferred_element_type=F32)


    own_queries = all_ref[slot, :q_rows]
    inverse = column_of(norm_c / totals_ref[slot, :1])
    inverse = jnp.concatenate([inverse] * (i_rows // LANES), axis=1)
    target = jnp.concatenate([column_of(pos_ref[...])] * (i_rows // LANES), axis=1)
    target = target - lax.broadcasted_iota(jnp.int32, (q_rows, i_rows), 1)

    def add_keys(t, d_queries):
        keys = all_ref[t, q_rows : q_rows + i_rows]
        shares = jnp.exp2(EXP_SCALE * contract_last(own_queries, keys)) * inverse
        weights = (shares - jnp.where(target == order[t] * i_rows, norm_c, 0.0)).astype(BF16)
        return d_queries + jnp.dot(weights, keys, preferred_element_type=F32)

    d_keys = jnp.zeros((i_rows, LANES), F32)
    d_queries = jnp.zeros((q_rows, LANES), F32)
    for r in range(ranks):
        d_keys = add_queries(r, d_keys)
        d_queries = add_keys(r, d_queries)

    d_key_outer = outer_grad(LOGIT_SCALE * d_keys, outers_ref[1])
    d_query_outer = outer_grad(LOGIT_SCALE * d_queries, outers_ref[0])
    d_query_outer_ref[...] = d_query_outer

    def split(query_ref, key_ref):
        query_ref[:q_rows] = d_query_outer
        query_ref[q_rows:] = pooled_ref[...]
        key_ref[:i_rows] = d_key_outer
        key_ref[i_rows:] = feats_ref[...]

    @pl.when(core == 0)
    def _():
        split(keep_ref, send_ref)

    @pl.when(core != 0)
    def _():
        split(send_ref, keep_ref)


def back_kernel(keep_ref, received_ref, hidden_ref, slope_ref, first_ref, second_ref, grads_ref):
    h = second_ref.shape[0]
    rows = keep_ref.shape[0] // 2
    second = second_ref[...]
    hidden_t, slope = forward(received_ref[rows:], first_ref[...])
    first_mine, second_mine = backward(keep_ref[rows:], hidden_ref[...], slope_ref[...], keep_ref[:rows], second)
    first_other, second_other = backward(received_ref[rows:], hidden_t, slope, received_ref[:rows], second)
    grads_ref[h:] = (second_mine + second_other).astype(BF16)
    first_grad = (first_mine + first_other).astype(BF16)
    for j in range(h // LANES):
        grads_ref[j * LANES : (j + 1) * LANES] = first_grad[:, j * LANES : (j + 1) * LANES]


def rows_kernel(
    tally_ref, counts_ref, pooled_ref, d_outer_ref, qw1_ref, qw2_ref, table_ref, state_ref, new_ref
):
    pre = jnp.dot(pooled_ref[...], qw1_ref[...], preferred_element_type=F32)
    sigma = jax.nn.sigmoid(pre)
    d_hidden = contract_last(d_outer_ref[...], qw2_ref[...])
    d_pre = (d_hidden * (sigma * (1.0 + pre * (1.0 - sigma)))).astype(BF16)
    d_x = contract_last(d_pre, qw1_ref[...])
    counts = column_of(counts_ref[...].astype(F32))
    pieces = three_pieces(d_x / counts)
    row_grads = add_pieces(jnp.dot(tally_ref[...], pieces, preferred_element_type=F32))
    mean = jnp.mean(row_grads * row_grads, axis=1, keepdims=True)
    acc = column_of(state_ref[...]) + mean
    new_ref[...] = table_ref[...] - LEARNING_RATE * row_grads / jnp.sqrt(acc)


def finish_kernel(
    where_ref, mine_ref, other_ref, q1_ref, q2_ref, i1_ref, i2_ref, first_ref, second_ref, sent
):
    core = where_ref[1]
    h = second_ref.shape[1]

    def write(query_source, item_source):
        copies = []
        for slot, (source_ref, first_hbm, second_hbm) in enumerate(
            ((query_source, q1_ref, q2_ref), (item_source, i1_ref, i2_ref))
        ):
            second_ref[slot] = source_ref[h:].astype(F32)
            copies.append(pltpu.make_async_copy(second_ref.at[slot], second_hbm, sent.at[slot, 0]))
            copies[-1].start()
            for j in range(0, h, LANES):
                first_ref[slot, :, j : j + LANES] = source_ref[j : j + LANES].astype(F32)
            copies.append(pltpu.make_async_copy(first_ref.at[slot], first_hbm, sent.at[slot, 1]))
            copies[-1].start()
        for copy in copies:
            copy.wait()

    @pl.when(core == 0)
    def _():
        write(mine_ref, other_ref)

    @pl.when(core != 0)
    def _():
        write(other_ref, mine_ref)


VMEM = pl.BlockSpec(memory_space=pltpu.VMEM)
SMEM = pl.BlockSpec(memory_space=pltpu.SMEM)
HBM = pl.BlockSpec(memory_space=pltpu.HBM)


def call(kernel, out_shape, operands, in_specs=None, out_specs=None, scratch=(), flops=0, limit=32):
    return pl.pallas_call(
        kernel,
        out_shape=out_shape,
        in_specs=in_specs or [VMEM] * len(operands),
        out_specs=out_specs or jax.tree.map(lambda _: VMEM, out_shape),
        scratch_shapes=list(scratch),
        compiler_params=pltpu.CompilerParams(vmem_limit_bytes=limit * 2**20),
        cost_estimate=pl.CostEstimate(flops=flops, bytes_accessed=2**20, transcendentals=0),
    )(*operands)


def exchange(values, axes):
    return lax.all_to_all(values, axes, 0, 0, tiled=True)


def per_device(rows, state, bag_ids, bag_counts, item_feats, positives, q_w1, q_w2, i_w1, i_w2):
    group = ("ya", "xl", "yb")
    block = ("zp", "xh", "xl", "ya", "yb")
    strided = ("zb", "zc", "za")
    struct = jax.ShapeDtypeStruct
    ranks = lax.axis_size(group)
    spread = lax.axis_size(block)
    table = rows[0]
    feats = item_feats[0]
    q_rows, e = bag_ids.shape[1], table.shape[1]
    i_rows = feats.shape[0]
    h = q_w2.shape[0]
    blk_axes = ("ya", "yb", "xl")
    where = jnp.stack(
        [lax.axis_index(group), lax.axis_index("c"), lax.axis_index(blk_axes)]
    ).astype(jnp.int32)
    sizes = [lax.axis_size(axis) for axis in blk_axes]
    numbers = np.arange(ranks).reshape(sizes).transpose([blk_axes.index(axis) for axis in group])
    order = [int(number) for number in numbers.reshape(-1)]

    ids = bag_ids[0].T
    arguments = [ids, bag_counts, positives, table, feats, q_w1, q_w2, i_w1, i_w2]
    arguments = [pltpu.with_memory_space_constraint(a, pltpu.HBM) for a in arguments]
    payload, pooled, tally, outers = call(
        front_kernel,
        [
            struct((ranks, q_rows + i_rows + CODE_ROWS, e), BF16),
            struct((q_rows, e), BF16),
            struct((table.shape[0], q_rows), BF16),
            struct((2, q_rows, e), F32),
        ],
        arguments,
        in_specs=[HBM] * len(arguments),
        scratch=[pltpu.VMEM(a.shape, a.dtype) for a in arguments]
        + [pltpu.SemaphoreType.DMA((len(arguments),))],
    )
    payload, where = lax.optimization_barrier((payload, where))
    everyone = exchange(payload, group)
    d_query_outer, keep, send = call(
        functools.partial(middle_kernel, order),
        [struct((q_rows, e), BF16), struct((2 * q_rows, e), BF16), struct((2 * q_rows, e), BF16)],
        [where, everyone, positives, outers, pooled, feats],
        in_specs=[SMEM] + [VMEM] * 5,
        scratch=[pltpu.VMEM((ranks, 8, q_rows), F32), pltpu.VMEM((ranks, 8, q_rows), jnp.int32)],
    )
    swap = [(0, 1), (1, 0)]
    received = lax.ppermute(send, "c", swap)
    prepared = call(
        prepare_kernel,
        [struct((h, q_rows), BF16), struct((q_rows, h), F32), struct((e, h), BF16), struct((h, e), BF16)],
        [where, keep, q_w1, q_w2, i_w1, i_w2],
        in_specs=[SMEM] + [VMEM] * 5,
        flops=2**28,
    )
    grads = call(back_kernel, struct((2 * h, e), BF16), [keep, received, *prepared])
    new_rows = call(
        rows_kernel,
        struct(table.shape, F32),
        [tally, bag_counts, pooled, d_query_outer, q_w1, q_w2, table, state],
        flops=2**30,
    )
    chip_sum = grads.reshape(spread, 2 * h // spread, e)
    mine = jnp.sum(exchange(chip_sum, block).astype(F32), axis=0).astype(BF16)
    copies = jnp.broadcast_to(mine, (lax.axis_size(strided),) + mine.shape)
    mine = jnp.sum(exchange(copies, strided).astype(F32), axis=0).astype(BF16)
    copies = jnp.broadcast_to(mine, (spread,) + mine.shape)
    tower = exchange(copies, block).reshape(2 * h, e)
    other = lax.ppermute(tower, "c", swap)
    sums = call(
        finish_kernel,
        [struct((e, h), F32), struct((h, e), F32), struct((e, h), F32), struct((h, e), F32)],
        [where, tower, other],
        in_specs=[SMEM, VMEM, VMEM],
        out_specs=[HBM] * 4,
        scratch=[
            pltpu.VMEM((2, e, h), F32),
            pltpu.VMEM((2, h, e), F32),
            pltpu.SemaphoreType.DMA((2, 2)),
        ],
    )
    return (new_rows[None], *sums)


def solution(mesh):
    blk_axes = ("ya", "yb", "xl")
    rep_axes = ("za", "zb", "zc", "zp", "xh", "c")
    parts = []
    for size, axes in zip(mesh.devices.shape, (blk_axes, rep_axes)):
        bits = size.bit_length() - 1
        parts += [1] * (len(axes) - bits) + [2] * bits
    fine = Mesh(mesh.devices.reshape(parts), blk_axes + rep_axes)
    in_specs = (
        P(rep_axes, blk_axes, None),
        P(rep_axes, blk_axes),
        P(rep_axes, blk_axes, None),
        P(rep_axes, blk_axes),
        P(rep_axes, blk_axes, None),
        P(rep_axes, blk_axes),
        P(),
        P(),
        P(),
        P(),
    )
    out_specs = (P(rep_axes, blk_axes, None), P(), P(), P(), P())
    return jax.shard_map(
        per_device, mesh=fine, in_specs=in_specs, out_specs=out_specs, check_vma=False
    )
```

```python
import functools

import jax
import jax.numpy as jnp
import numpy as np
from jax import lax
from jax.experimental import pallas as pl
from jax.experimental.pallas import tpu as pltpu
from jax.sharding import Mesh, PartitionSpec as P

LOGIT_SCALE = 20.0
EXP_SCALE = 28.853900817779268
LEARNING_RATE = 0.5
NORM_EPS = 1e-06

BF16 = jnp.bfloat16
F32 = jnp.float32

CODE_ROWS = 16
LANES = 128


def contract_lead(left, right):
    return lax.dot_general(left, right, (((0,), (0,)), ((), ())), preferred_element_type=F32)


def contract_last(left, right):
    return lax.dot_general(left, right, (((1,), (1,)), ((), ())), preferred_element_type=F32)


def column_of(row):
    return jnp.transpose(jnp.broadcast_to(row, (LANES, row.shape[1])))


def three_pieces(values):
    high = values.astype(BF16)
    rest = values - high.astype(F32)
    middle = rest.astype(BF16)
    low = (rest - middle.astype(F32)).astype(BF16)
    return jnp.concatenate([high, middle, low], axis=1)


def add_pieces(product):
    return (product[:, 2 * LANES :] + product[:, LANES : 2 * LANES]) + product[:, :LANES]


def radius_of(outer):
    return jnp.sqrt(jnp.sum(outer * outer, axis=1, keepdims=True) + NORM_EPS)


def front_kernel(
    ids_hbm, counts_hbm, pos_hbm, table_hbm, feats_hbm, qw1_hbm, qw2_hbm, iw1_hbm, iw2_hbm,
    payload_ref, pooled_ref, tally_ref, outers_ref,
    ids_ref, counts_ref, pos_ref, table_ref, feats_ref, qw1_ref, qw2_ref, iw1_ref, iw2_ref, arrived,
):
    sources = (ids_hbm, counts_hbm, table_hbm, qw1_hbm, feats_hbm, iw1_hbm, qw2_hbm, iw2_hbm, pos_hbm)
    targets = (ids_ref, counts_ref, table_ref, qw1_ref, feats_ref, iw1_ref, qw2_ref, iw2_ref, pos_ref)
    copies = [
        pltpu.make_async_copy(source, target, arrived.at[i])
        for i, (source, target) in enumerate(zip(sources, targets))
    ]
    for copy in copies:
        copy.start()

    members, q_rows = ids_ref.shape
    table_rows = table_ref.shape[0]
    copies[0].wait()
    copies[1].wait()
    counts = counts_ref[...]
    rows = lax.broadcasted_iota(jnp.int32, (table_rows, q_rows), 0)
    tally = jnp.zeros((table_rows, q_rows), F32)
    for m in range(members):
        live = jnp.where(counts > m, ids_ref[m : m + 1], -1)
        tally = tally + jnp.where(live == rows, 1.0, 0.0)
    tally = tally.astype(BF16)
    tally_ref[...] = tally
    copies[2].wait()
    product = contract_lead(tally, three_pieces(table_ref[...]))
    pooled = (add_pieces(product) / column_of(counts.astype(F32))).astype(BF16)
    pooled_ref[...] = pooled

    def tower(inputs, first, second, slot):
        copies[first].wait()
        pre = jnp.dot(inputs, targets[first][...], preferred_element_type=F32)
        hidden = (pre * jax.nn.sigmoid(pre)).astype(BF16)
        copies[second].wait()
        outer = jnp.dot(hidden, targets[second][...], preferred_element_type=F32)
        outers_ref[slot] = outer
        return (outer / radius_of(outer)).astype(BF16)

    queries = tower(pooled, 3, 6, 0)
    copies[4].wait()
    keys = tower(feats_ref[...], 5, 7, 1)
    copies[8].wait()
    pos = pos_ref[...]
    digits = jnp.concatenate([pos // LANES, pos % LANES], axis=0).astype(F32)
    spread = jnp.concatenate(
        [digits[:, i * LANES : (i + 1) * LANES] for i in range(q_rows // LANES)]
        + [jnp.zeros((CODE_ROWS - 2 * (q_rows // LANES), LANES), F32)],
        axis=0,
    ).astype(BF16)
    for copy in range(payload_ref.shape[0]):
        payload_ref[copy, :q_rows] = queries
        payload_ref[copy, q_rows : 2 * q_rows] = keys
        payload_ref[copy, 2 * q_rows :] = spread


def backward(inputs, hidden_t, slope, d_outer, second):
    d_pre = (contract_last(d_outer, second) * slope).astype(BF16)
    return contract_lead(inputs, d_pre), jnp.dot(hidden_t, d_outer, preferred_element_type=F32)


def forward(inputs, first):
    pre = jnp.dot(inputs, first, preferred_element_type=F32)
    sigma = jax.nn.sigmoid(pre)
    return jnp.transpose((pre * sigma).astype(BF16)), sigma * (1.0 + pre * (1.0 - sigma))


def prepare_kernel(
    where_ref, keep_ref, qw1_ref, qw2_ref, iw1_ref, iw2_ref,
    hidden_ref, slope_ref, first_ref, second_ref,
):
    core = where_ref[1]

    @pl.when(core == 0)
    def _():
        first_ref[...] = qw1_ref[...]
        second_ref[...] = qw2_ref[...]

    @pl.when(core != 0)
    def _():
        first_ref[...] = iw1_ref[...]
        second_ref[...] = iw2_ref[...]

    hidden_ref[...], slope_ref[...] = forward(keep_ref[keep_ref.shape[0] // 2 :], first_ref[...])


def outer_grad(d_unit, outer):
    radius = radius_of(outer)
    unit = outer / radius
    along = jnp.sum(unit * d_unit, axis=1, keepdims=True)
    return ((d_unit - unit * along) / radius).astype(BF16)


def middle_kernel(
    order, where_ref, all_ref, pos_ref, outers_ref, pooled_ref, feats_ref,
    d_query_outer_ref, keep_ref, send_ref,
    totals_ref, codes_ref, by_item_ref, by_query_ref,
):
    ranks = all_ref.shape[0]
    q_rows = outers_ref.shape[1]
    i_rows = outers_ref.shape[1]
    slot = where_ref[0]
    core = where_ref[1]
    item_start = where_ref[2] * i_rows
    norm_c = 1.0 / (q_rows * ranks)

    own_keys = all_ref[slot, q_rows : q_rows + i_rows]
    own_queries = all_ref[slot, :q_rows]

    def powers(left, right):
        return jnp.exp2(EXP_SCALE * contract_last(left, right))

    def fold(values):
        return jnp.sum(values.reshape(values.shape[0] // 8, 8, values.shape[1]), axis=0)

    own_sums = jnp.zeros((q_rows, LANES), F32)
    for s in range(ranks):
        by_item_ref[s] = powers(own_keys, all_ref[s, :q_rows])
        totals_ref[s] = fold(by_item_ref[s])
        by_query = powers(own_queries, all_ref[s, q_rows : q_rows + i_rows])
        by_query_ref[s] = by_query
        for i in range(0, i_rows, LANES):
            own_sums = own_sums + by_query[:, i : i + LANES]
        digits = all_ref[s, q_rows + i_rows :].astype(F32)
        chunks = q_rows // LANES
        code = jnp.concatenate(
            [digits[2 * i : 2 * i + 1] * LANES + digits[2 * i + 1 : 2 * i + 2] for i in range(chunks)],
            axis=1,
        )
        codes_ref[s] = jnp.broadcast_to(code.astype(jnp.int32), (8, q_rows))

    for j in range(1, ranks):
        s = lax.rem(slot + j, ranks)
        queries = all_ref[s, :q_rows]
        partial = totals_ref[s]
        for i in range(1, ranks):
            t = lax.rem(slot + i, ranks)
            partial = partial + fold(powers(all_ref[t, q_rows : q_rows + i_rows], queries))
        totals_ref[s] = jnp.broadcast_to(jnp.sum(partial, axis=0, keepdims=True), (8, q_rows))
    own_total = jnp.broadcast_to(jnp.sum(own_sums, axis=1, keepdims=True), (q_rows, LANES))
    totals_ref[slot] = jnp.transpose(own_total)[:8]

    item = item_start + lax.broadcasted_iota(jnp.int32, (i_rows, q_rows), 0)
    inverse = jnp.concatenate([norm_c / own_total] * (i_rows // LANES), axis=1)
    target = jnp.concatenate([column_of(pos_ref[...])] * (i_rows // LANES), axis=1)
    target = target - lax.broadcasted_iota(jnp.int32, (q_rows, i_rows), 1)
    d_keys = jnp.zeros((i_rows, LANES), F32)
    d_queries = jnp.zeros((q_rows, LANES), F32)
    for r in range(ranks):
        shares = by_item_ref[r] * (norm_c / totals_ref[r, :1])
        weights = (shares - jnp.where(codes_ref[r, :1] == item, norm_c, 0.0)).astype(BF16)
        d_keys = d_keys + jnp.dot(weights, all_ref[r, :q_rows], preferred_element_type=F32)
        shares = by_query_ref[r] * inverse
        weights = (shares - jnp.where(target == order[r] * i_rows, norm_c, 0.0)).astype(BF16)
        keys = all_ref[r, q_rows : q_rows + i_rows]
        d_queries = d_queries + jnp.dot(weights, keys, preferred_element_type=F32)
    d_key_outer = outer_grad(LOGIT_SCALE * d_keys, outers_ref[1])
    d_query_outer = outer_grad(LOGIT_SCALE * d_queries, outers_ref[0])
    d_query_outer_ref[...] = d_query_outer

    def split(query_ref, key_ref):
        query_ref[:q_rows] = d_query_outer
        query_ref[q_rows:] = pooled_ref[...]
        key_ref[:i_rows] = d_key_outer
        key_ref[i_rows:] = feats_ref[...]

    @pl.when(core == 0)
    def _():
        split(keep_ref, send_ref)

    @pl.when(core != 0)
    def _():
        split(send_ref, keep_ref)


def back_kernel(keep_ref, received_ref, hidden_ref, slope_ref, first_ref, second_ref, grads_ref):
    h = second_ref.shape[0]
    rows = keep_ref.shape[0] // 2
    second = second_ref[...]
    hidden_t, slope = forward(received_ref[rows:], first_ref[...])
    first_mine, second_mine = backward(keep_ref[rows:], hidden_ref[...], slope_ref[...], keep_ref[:rows], second)
    first_other, second_other = backward(received_ref[rows:], hidden_t, slope, received_ref[:rows], second)
    grads_ref[h:] = (second_mine + second_other).astype(BF16)
    first_grad = (first_mine + first_other).astype(BF16)
    for j in range(h // LANES):
        grads_ref[j * LANES : (j + 1) * LANES] = first_grad[:, j * LANES : (j + 1) * LANES]


def rows_kernel(
    tally_ref, counts_ref, pooled_ref, d_outer_ref, qw1_ref, qw2_ref, table_ref, state_ref, new_ref
):
    pre = jnp.dot(pooled_ref[...], qw1_ref[...], preferred_element_type=F32)
    sigma = jax.nn.sigmoid(pre)
    d_hidden = contract_last(d_outer_ref[...], qw2_ref[...])
    d_pre = (d_hidden * (sigma * (1.0 + pre * (1.0 - sigma)))).astype(BF16)
    d_x = contract_last(d_pre, qw1_ref[...])
    counts = column_of(counts_ref[...].astype(F32))
    pieces = three_pieces(d_x / counts)
    row_grads = add_pieces(jnp.dot(tally_ref[...], pieces, preferred_element_type=F32))
    mean = jnp.mean(row_grads * row_grads, axis=1, keepdims=True)
    acc = column_of(state_ref[...]) + mean
    new_ref[...] = table_ref[...] - LEARNING_RATE * row_grads / jnp.sqrt(acc)


def finish_kernel(
    where_ref, mine_ref, other_ref, q1_ref, q2_ref, i1_ref, i2_ref, first_ref, second_ref, sent
):
    core = where_ref[1]
    h = second_ref.shape[1]

    def write(query_source, item_source):
        copies = []
        for slot, (source_ref, first_hbm, second_hbm) in enumerate(
            ((query_source, q1_ref, q2_ref), (item_source, i1_ref, i2_ref))
        ):
            second_ref[slot] = source_ref[h:].astype(F32)
            copies.append(pltpu.make_async_copy(second_ref.at[slot], second_hbm, sent.at[slot, 0]))
            copies[-1].start()
            for j in range(0, h, LANES):
                first_ref[slot, :, j : j + LANES] = source_ref[j : j + LANES].astype(F32)
            copies.append(pltpu.make_async_copy(first_ref.at[slot], first_hbm, sent.at[slot, 1]))
            copies[-1].start()
        for copy in copies:
            copy.wait()

    @pl.when(core == 0)
    def _():
        write(mine_ref, other_ref)

    @pl.when(core != 0)
    def _():
        write(other_ref, mine_ref)


VMEM = pl.BlockSpec(memory_space=pltpu.VMEM)
SMEM = pl.BlockSpec(memory_space=pltpu.SMEM)
HBM = pl.BlockSpec(memory_space=pltpu.HBM)


def call(kernel, out_shape, operands, in_specs=None, out_specs=None, scratch=(), flops=0, limit=32):
    return pl.pallas_call(
        kernel,
        out_shape=out_shape,
        in_specs=in_specs or [VMEM] * len(operands),
        out_specs=out_specs or jax.tree.map(lambda _: VMEM, out_shape),
        scratch_shapes=list(scratch),
        compiler_params=pltpu.CompilerParams(vmem_limit_bytes=limit * 2**20),
        cost_estimate=pl.CostEstimate(flops=flops, bytes_accessed=2**20, transcendentals=0),
    )(*operands)


def exchange(values, axes):
    return lax.all_to_all(values, axes, 0, 0, tiled=True)


def per_device(rows, state, bag_ids, bag_counts, item_feats, positives, q_w1, q_w2, i_w1, i_w2):
    group = ("yb", "xl", "ya")
    block = ("zp", "ya", "yb", "xh", "xl")
    strided = ("zb", "zc", "za")
    struct = jax.ShapeDtypeStruct
    ranks = lax.axis_size(group)
    spread = lax.axis_size(block)
    table = rows[0]
    feats = item_feats[0]
    q_rows, e = bag_ids.shape[1], table.shape[1]
    i_rows = feats.shape[0]
    h = q_w2.shape[0]
    blk_axes = ("ya", "yb", "xl")
    where = jnp.stack(
        [lax.axis_index(group), lax.axis_index("c"), lax.axis_index(blk_axes)]
    ).astype(jnp.int32)
    sizes = [lax.axis_size(axis) for axis in blk_axes]
    numbers = np.arange(ranks).reshape(sizes).transpose([blk_axes.index(axis) for axis in group])
    order = [int(number) for number in numbers.reshape(-1)]

    ids = bag_ids[0].T
    arguments = [ids, bag_counts, positives, table, feats, q_w1, q_w2, i_w1, i_w2]
    arguments = [pltpu.with_memory_space_constraint(a, pltpu.HBM) for a in arguments]
    payload, pooled, tally, outers = call(
        front_kernel,
        [
            struct((ranks, q_rows + i_rows + CODE_ROWS, e), BF16),
            struct((q_rows, e), BF16),
            struct((table.shape[0], q_rows), BF16),
            struct((2, q_rows, e), F32),
        ],
        arguments,
        in_specs=[HBM] * len(arguments),
        scratch=[pltpu.VMEM(a.shape, a.dtype) for a in arguments]
        + [pltpu.SemaphoreType.DMA((len(arguments),))],
    )
    payload, where = lax.optimization_barrier((payload, where))
    everyone = exchange(payload, group)
    d_query_outer, keep, send = call(
        functools.partial(middle_kernel, order),
        [struct((q_rows, e), BF16), struct((2 * q_rows, e), BF16), struct((2 * q_rows, e), BF16)],
        [where, everyone, positives, outers, pooled, feats],
        in_specs=[SMEM] + [VMEM] * 5,
        scratch=[
            pltpu.VMEM((ranks, 8, q_rows), F32),
            pltpu.VMEM((ranks, 8, q_rows), jnp.int32),
            pltpu.VMEM((ranks, i_rows, q_rows), F32),
            pltpu.VMEM((ranks, q_rows, i_rows), F32),
        ],
    )
    swap = [(0, 1), (1, 0)]
    received = lax.ppermute(send, "c", swap)
    prepared = call(
        prepare_kernel,
        [struct((h, q_rows), BF16), struct((q_rows, h), F32), struct((e, h), BF16), struct((h, e), BF16)],
        [where, keep, q_w1, q_w2, i_w1, i_w2],
        in_specs=[SMEM] + [VMEM] * 5,
        flops=2**28,
    )
    grads = call(back_kernel, struct((2 * h, e), BF16), [keep, received, *prepared])
    new_rows = call(
        rows_kernel,
        struct(table.shape, F32),
        [tally, bag_counts, pooled, d_query_outer, q_w1, q_w2, table, state],
        flops=2**30,
    )
    chip_sum = grads.reshape(spread, 2 * h // spread, e)
    mine = jnp.sum(exchange(chip_sum, block).astype(F32), axis=0).astype(BF16)
    copies = jnp.broadcast_to(mine, (lax.axis_size(strided),) + mine.shape)
    mine = jnp.sum(exchange(copies, strided).astype(F32), axis=0).astype(BF16)
    copies = jnp.broadcast_to(mine, (spread,) + mine.shape)
    tower = exchange(copies, block).reshape(2 * h, e)
    other = lax.ppermute(tower, "c", swap)
    sums = call(
        finish_kernel,
        [struct((e, h), F32), struct((h, e), F32), struct((e, h), F32), struct((h, e), F32)],
        [where, tower, other],
        in_specs=[SMEM, VMEM, VMEM],
        out_specs=[HBM] * 4,
        scratch=[
            pltpu.VMEM((2, e, h), F32),
            pltpu.VMEM((2, h, e), F32),
            pltpu.SemaphoreType.DMA((2, 2)),
        ],
    )
    return (new_rows[None], *sums)


def solution(mesh):
    blk_axes = ("ya", "yb", "xl")
    rep_axes = ("za", "zb", "zc", "zp", "xh", "c")
    parts = []
    for size, axes in zip(mesh.devices.shape, (blk_axes, rep_axes)):
        bits = size.bit_length() - 1
        parts += [1] * (len(axes) - bits) + [2] * bits
    fine = Mesh(mesh.devices.reshape(parts), blk_axes + rep_axes)
    in_specs = (
        P(rep_axes, blk_axes, None),
        P(rep_axes, blk_axes),
        P(rep_axes, blk_axes, None),
        P(rep_axes, blk_axes),
        P(rep_axes, blk_axes, None),
        P(rep_axes, blk_axes),
        P(),
        P(),
        P(),
        P(),
    )
    out_specs = (P(rep_axes, blk_axes, None), P(), P(), P(), P())
    return jax.shard_map(
        per_device, mesh=fine, in_specs=in_specs, out_specs=out_specs, check_vma=False
    )
```

```python
import functools

import jax
import jax.numpy as jnp
import numpy as np
from jax import lax
from jax.experimental import pallas as pl
from jax.experimental.pallas import tpu as pltpu
from jax.sharding import Mesh, PartitionSpec as P

LOGIT_SCALE = 20.0
EXP_SCALE = 28.853900817779268
LEARNING_RATE = 0.5
NORM_EPS = 1e-06

BF16 = jnp.bfloat16
F32 = jnp.float32

CODE_ROWS = 16
LANES = 128


def contract_lead(left, right):
    return lax.dot_general(left, right, (((0,), (0,)), ((), ())), preferred_element_type=F32)


def contract_last(left, right):
    return lax.dot_general(left, right, (((1,), (1,)), ((), ())), preferred_element_type=F32)


def column_of(row):
    return jnp.transpose(jnp.broadcast_to(row, (LANES, row.shape[1])))


def three_pieces(values):
    high = values.astype(BF16)
    rest = values - high.astype(F32)
    middle = rest.astype(BF16)
    low = (rest - middle.astype(F32)).astype(BF16)
    return jnp.concatenate([high, middle, low], axis=1)


def add_pieces(product):
    return (product[:, 2 * LANES :] + product[:, LANES : 2 * LANES]) + product[:, :LANES]


def radius_of(outer):
    return jnp.sqrt(jnp.sum(outer * outer, axis=1, keepdims=True) + NORM_EPS)


def front_kernel(
    ids_hbm, counts_hbm, pos_hbm, table_hbm, feats_hbm, qw1_hbm, qw2_hbm, iw1_hbm, iw2_hbm,
    payload_ref, pooled_ref, tally_ref, outers_ref,
    ids_ref, counts_ref, pos_ref, table_ref, feats_ref, qw1_ref, qw2_ref, iw1_ref, iw2_ref, arrived,
):
    sources = (ids_hbm, counts_hbm, table_hbm, qw1_hbm, feats_hbm, iw1_hbm, qw2_hbm, iw2_hbm, pos_hbm)
    targets = (ids_ref, counts_ref, table_ref, qw1_ref, feats_ref, iw1_ref, qw2_ref, iw2_ref, pos_ref)
    copies = [
        pltpu.make_async_copy(source, target, arrived.at[i])
        for i, (source, target) in enumerate(zip(sources, targets))
    ]
    for copy in copies:
        copy.start()

    def tower(inputs, first, second, slot):
        pre = jnp.dot(inputs, targets[first][...], preferred_element_type=F32)
        hidden = (pre * jax.nn.sigmoid(pre)).astype(BF16)
        outer = jnp.dot(hidden, targets[second][...], preferred_element_type=F32)
        outers_ref[slot] = outer
        return (outer / radius_of(outer)).astype(BF16)

    members, q_rows = ids_ref.shape
    table_rows = table_ref.shape[0]
    copies[0].wait()
    copies[1].wait()
    counts = counts_ref[...]
    rows = lax.broadcasted_iota(jnp.int32, (table_rows, q_rows), 0)
    tally = jnp.zeros((table_rows, q_rows), F32)
    for m in range(members):
        live = jnp.where(counts > m, ids_ref[m : m + 1], -1)
        tally = tally + jnp.where(live == rows, 1.0, 0.0)
    tally = tally.astype(BF16)
    tally_ref[...] = tally
    for copy in copies[2:]:
        copy.wait()
    keys = tower(feats_ref[...], 5, 7, 1)
    product = contract_lead(tally, three_pieces(table_ref[...]))
    pooled = (add_pieces(product) / column_of(counts.astype(F32))).astype(BF16)
    pooled_ref[...] = pooled

    queries = tower(pooled, 3, 6, 0)
    pos = pos_ref[...]
    digits = jnp.concatenate([pos // LANES, pos % LANES], axis=0).astype(F32)
    spread = jnp.concatenate(
        [digits[:, i * LANES : (i + 1) * LANES] for i in range(q_rows // LANES)]
        + [jnp.zeros((CODE_ROWS - 2 * (q_rows // LANES), LANES), F32)],
        axis=0,
    ).astype(BF16)
    for copy in range(payload_ref.shape[0]):
        payload_ref[copy, :q_rows] = queries
        payload_ref[copy, q_rows : 2 * q_rows] = keys
        payload_ref[copy, 2 * q_rows :] = spread


def backward(inputs, hidden_t, slope, d_outer, second):
    d_pre = (contract_last(d_outer, second) * slope).astype(BF16)
    return contract_lead(inputs, d_pre), jnp.dot(hidden_t, d_outer, preferred_element_type=F32)


def forward(inputs, first):
    pre = jnp.dot(inputs, first, preferred_element_type=F32)
    sigma = jax.nn.sigmoid(pre)
    return jnp.transpose((pre * sigma).astype(BF16)), sigma * (1.0 + pre * (1.0 - sigma))


def prepare_kernel(
    where_ref, keep_ref, qw1_ref, qw2_ref, iw1_ref, iw2_ref,
    hidden_ref, slope_ref, first_ref, second_ref,
):
    core = where_ref[1]

    @pl.when(core == 0)
    def _():
        first_ref[...] = qw1_ref[...]
        second_ref[...] = qw2_ref[...]

    @pl.when(core != 0)
    def _():
        first_ref[...] = iw1_ref[...]
        second_ref[...] = iw2_ref[...]

    hidden_ref[...], slope_ref[...] = forward(keep_ref[keep_ref.shape[0] // 2 :], first_ref[...])


def outer_grad(d_unit, outer):
    radius = radius_of(outer)
    unit = outer / radius
    along = jnp.sum(unit * d_unit, axis=1, keepdims=True)
    return ((d_unit - unit * along) / radius).astype(BF16)


def middle_kernel(
    order, where_ref, all_ref, pos_ref, outers_ref, pooled_ref, feats_ref,
    d_query_outer_ref, keep_ref, send_ref,
    totals_ref, codes_ref, by_item_ref, by_query_ref,
):
    ranks = all_ref.shape[0]
    q_rows = outers_ref.shape[1]
    i_rows = outers_ref.shape[1]
    slot = where_ref[0]
    core = where_ref[1]
    item_start = where_ref[2] * i_rows
    norm_c = 1.0 / (q_rows * ranks)

    own_keys = all_ref[slot, q_rows : q_rows + i_rows]
    own_queries = all_ref[slot, :q_rows]

    def powers(left, right):
        return jnp.exp2(EXP_SCALE * contract_last(left, right))

    def fold(values):
        return jnp.sum(values.reshape(values.shape[0] // 8, 8, values.shape[1]), axis=0)

    own_sums = jnp.zeros((q_rows, LANES), F32)
    for s in range(ranks):
        by_item_ref[s] = powers(own_keys, all_ref[s, :q_rows])
        totals_ref[s] = fold(by_item_ref[s])
        by_query = powers(own_queries, all_ref[s, q_rows : q_rows + i_rows])
        by_query_ref[s] = by_query
        for i in range(0, i_rows, LANES):
            own_sums = own_sums + by_query[:, i : i + LANES]
        digits = all_ref[s, q_rows + i_rows :].astype(F32)
        chunks = q_rows // LANES
        code = jnp.concatenate(
            [digits[2 * i : 2 * i + 1] * LANES + digits[2 * i + 1 : 2 * i + 2] for i in range(chunks)],
            axis=1,
        )
        codes_ref[s] = jnp.broadcast_to(code.astype(jnp.int32), (8, q_rows))

    for j in range(1, ranks):
        s = lax.rem(slot + j, ranks)
        queries = all_ref[s, :q_rows]
        partial = totals_ref[s]
        for i in range(1, ranks):
            t = lax.rem(slot + i, ranks)
            partial = partial + fold(powers(all_ref[t, q_rows : q_rows + i_rows], queries))
        totals_ref[s] = jnp.broadcast_to(jnp.sum(partial, axis=0, keepdims=True), (8, q_rows))
    own_total = jnp.broadcast_to(jnp.sum(own_sums, axis=1, keepdims=True), (q_rows, LANES))
    totals_ref[slot] = jnp.transpose(own_total)[:8]

    item = item_start + lax.broadcasted_iota(jnp.int32, (i_rows, q_rows), 0)
    inverse = jnp.concatenate([norm_c / own_total] * (i_rows // LANES), axis=1)
    target = jnp.concatenate([column_of(pos_ref[...])] * (i_rows // LANES), axis=1)
    target = target - lax.broadcasted_iota(jnp.int32, (q_rows, i_rows), 1)
    d_keys = jnp.zeros((i_rows, LANES), F32)
    d_queries = jnp.zeros((q_rows, LANES), F32)
    for r in range(ranks):
        shares = by_item_ref[r] * (norm_c / totals_ref[r, :1])
        weights = (shares - jnp.where(codes_ref[r, :1] == item, norm_c, 0.0)).astype(BF16)
        d_keys = d_keys + jnp.dot(weights, all_ref[r, :q_rows], preferred_element_type=F32)
        shares = by_query_ref[r] * inverse
        weights = (shares - jnp.where(target == order[r] * i_rows, norm_c, 0.0)).astype(BF16)
        keys = all_ref[r, q_rows : q_rows + i_rows]
        d_queries = d_queries + jnp.dot(weights, keys, preferred_element_type=F32)
    d_key_outer = outer_grad(LOGIT_SCALE * d_keys, outers_ref[1])
    d_query_outer = outer_grad(LOGIT_SCALE * d_queries, outers_ref[0])
    d_query_outer_ref[...] = d_query_outer

    def split(query_ref, key_ref):
        query_ref[:q_rows] = d_query_outer
        query_ref[q_rows:] = pooled_ref[...]
        key_ref[:i_rows] = d_key_outer
        key_ref[i_rows:] = feats_ref[...]

    @pl.when(core == 0)
    def _():
        split(keep_ref, send_ref)

    @pl.when(core != 0)
    def _():
        split(send_ref, keep_ref)


def back_kernel(keep_ref, received_ref, hidden_ref, slope_ref, first_ref, second_ref, grads_ref):
    h = second_ref.shape[0]
    rows = keep_ref.shape[0] // 2
    second = second_ref[...]
    hidden_t, slope = forward(received_ref[rows:], first_ref[...])
    first_mine, second_mine = backward(keep_ref[rows:], hidden_ref[...], slope_ref[...], keep_ref[:rows], second)
    first_other, second_other = backward(received_ref[rows:], hidden_t, slope, received_ref[:rows], second)
    grads_ref[h:] = (second_mine + second_other).astype(BF16)
    first_grad = (first_mine + first_other).astype(BF16)
    for j in range(h // LANES):
        grads_ref[j * LANES : (j + 1) * LANES] = first_grad[:, j * LANES : (j + 1) * LANES]


def rows_kernel(
    tally_ref, counts_ref, pooled_ref, d_outer_ref, qw1_ref, qw2_ref, table_ref, state_ref, new_ref
):
    pre = jnp.dot(pooled_ref[...], qw1_ref[...], preferred_element_type=F32)
    sigma = jax.nn.sigmoid(pre)
    d_hidden = contract_last(d_outer_ref[...], qw2_ref[...])
    d_pre = (d_hidden * (sigma * (1.0 + pre * (1.0 - sigma)))).astype(BF16)
    d_x = contract_last(d_pre, qw1_ref[...])
    counts = column_of(counts_ref[...].astype(F32))
    pieces = three_pieces(d_x / counts)
    row_grads = add_pieces(jnp.dot(tally_ref[...], pieces, preferred_element_type=F32))
    mean = jnp.mean(row_grads * row_grads, axis=1, keepdims=True)
    acc = column_of(state_ref[...]) + mean
    new_ref[...] = table_ref[...] - LEARNING_RATE * row_grads / jnp.sqrt(acc)


def finish_kernel(
    where_ref, mine_ref, other_ref, q1_ref, q2_ref, i1_ref, i2_ref, first_ref, second_ref, sent
):
    core = where_ref[1]
    h = second_ref.shape[1]

    def write(query_source, item_source):
        copies = []
        for slot, (source_ref, first_hbm, second_hbm) in enumerate(
            ((query_source, q1_ref, q2_ref), (item_source, i1_ref, i2_ref))
        ):
            second_ref[slot] = source_ref[h:].astype(F32)
            copies.append(pltpu.make_async_copy(second_ref.at[slot], second_hbm, sent.at[slot, 0]))
            copies[-1].start()
            for j in range(0, h, LANES):
                first_ref[slot, :, j : j + LANES] = source_ref[j : j + LANES].astype(F32)
            copies.append(pltpu.make_async_copy(first_ref.at[slot], first_hbm, sent.at[slot, 1]))
            copies[-1].start()
        for copy in copies:
            copy.wait()

    @pl.when(core == 0)
    def _():
        write(mine_ref, other_ref)

    @pl.when(core != 0)
    def _():
        write(other_ref, mine_ref)


VMEM = pl.BlockSpec(memory_space=pltpu.VMEM)
SMEM = pl.BlockSpec(memory_space=pltpu.SMEM)
HBM = pl.BlockSpec(memory_space=pltpu.HBM)


def call(kernel, out_shape, operands, in_specs=None, out_specs=None, scratch=(), flops=0, limit=32):
    return pl.pallas_call(
        kernel,
        out_shape=out_shape,
        in_specs=in_specs or [VMEM] * len(operands),
        out_specs=out_specs or jax.tree.map(lambda _: VMEM, out_shape),
        scratch_shapes=list(scratch),
        compiler_params=pltpu.CompilerParams(vmem_limit_bytes=limit * 2**20),
        cost_estimate=pl.CostEstimate(flops=flops, bytes_accessed=2**20, transcendentals=0),
    )(*operands)


def exchange(values, axes):
    return lax.all_to_all(values, axes, 0, 0, tiled=True)


def per_device(rows, state, bag_ids, bag_counts, item_feats, positives, q_w1, q_w2, i_w1, i_w2):
    group = ("yb", "xl", "ya")
    block = ("zp", "ya", "yb", "xh", "xl")
    strided = ("zb", "zc", "za")
    struct = jax.ShapeDtypeStruct
    ranks = lax.axis_size(group)
    spread = lax.axis_size(block)
    table = rows[0]
    feats = item_feats[0]
    q_rows, e = bag_ids.shape[1], table.shape[1]
    i_rows = feats.shape[0]
    h = q_w2.shape[0]
    blk_axes = ("ya", "yb", "xl")
    where = jnp.stack(
        [lax.axis_index(group), lax.axis_index("c"), lax.axis_index(blk_axes)]
    ).astype(jnp.int32)
    sizes = [lax.axis_size(axis) for axis in blk_axes]
    numbers = np.arange(ranks).reshape(sizes).transpose([blk_axes.index(axis) for axis in group])
    order = [int(number) for number in numbers.reshape(-1)]

    ids = bag_ids[0].T
    arguments = [ids, bag_counts, positives, table, feats, q_w1, q_w2, i_w1, i_w2]
    arguments = [pltpu.with_memory_space_constraint(a, pltpu.HBM) for a in arguments]
    payload, pooled, tally, outers = call(
        front_kernel,
        [
            struct((ranks, q_rows + i_rows + CODE_ROWS, e), BF16),
            struct((q_rows, e), BF16),
            struct((table.shape[0], q_rows), BF16),
            struct((2, q_rows, e), F32),
        ],
        arguments,
        in_specs=[HBM] * len(arguments),
        scratch=[pltpu.VMEM(a.shape, a.dtype) for a in arguments]
        + [pltpu.SemaphoreType.DMA((len(arguments),))],
    )
    payload, where = lax.optimization_barrier((payload, where))
    everyone = exchange(payload, group)
    d_query_outer, keep, send = call(
        functools.partial(middle_kernel, order),
        [struct((q_rows, e), BF16), struct((2 * q_rows, e), BF16), struct((2 * q_rows, e), BF16)],
        [where, everyone, positives, outers, pooled, feats],
        in_specs=[SMEM] + [VMEM] * 5,
        scratch=[
            pltpu.VMEM((ranks, 8, q_rows), F32),
            pltpu.VMEM((ranks, 8, q_rows), jnp.int32),
            pltpu.VMEM((ranks, i_rows, q_rows), F32),
            pltpu.VMEM((ranks, q_rows, i_rows), F32),
        ],
    )
    swap = [(0, 1), (1, 0)]
    received = lax.ppermute(send, "c", swap)
    prepared = call(
        prepare_kernel,
        [struct((h, q_rows), BF16), struct((q_rows, h), F32), struct((e, h), BF16), struct((h, e), BF16)],
        [where, keep, q_w1, q_w2, i_w1, i_w2],
        in_specs=[SMEM] + [VMEM] * 5,
        flops=2**28,
    )
    grads = call(back_kernel, struct((2 * h, e), BF16), [keep, received, *prepared])
    new_rows = call(
        rows_kernel,
        struct(table.shape, F32),
        [tally, bag_counts, pooled, d_query_outer, q_w1, q_w2, table, state],
        flops=2**30,
    )
    chip_sum = grads.reshape(spread, 2 * h // spread, e)
    mine = jnp.sum(exchange(chip_sum, block).astype(F32), axis=0).astype(BF16)
    copies = jnp.broadcast_to(mine, (lax.axis_size(strided),) + mine.shape)
    mine = jnp.sum(exchange(copies, strided).astype(F32), axis=0).astype(BF16)
    copies = jnp.broadcast_to(mine, (spread,) + mine.shape)
    tower = exchange(copies, block).reshape(2 * h, e)
    other = lax.ppermute(tower, "c", swap)
    sums = call(
        finish_kernel,
        [struct((e, h), F32), struct((h, e), F32), struct((e, h), F32), struct((h, e), F32)],
        [where, tower, other],
        in_specs=[SMEM, VMEM, VMEM],
        out_specs=[HBM] * 4,
        scratch=[
            pltpu.VMEM((2, e, h), F32),
            pltpu.VMEM((2, h, e), F32),
            pltpu.SemaphoreType.DMA((2, 2)),
        ],
    )
    return (new_rows[None], *sums)


def solution(mesh):
    blk_axes = ("ya", "yb", "xl")
    rep_axes = ("za", "zb", "zc", "zp", "xh", "c")
    parts = []
    for size, axes in zip(mesh.devices.shape, (blk_axes, rep_axes)):
        bits = size.bit_length() - 1
        parts += [1] * (len(axes) - bits) + [2] * bits
    fine = Mesh(mesh.devices.reshape(parts), blk_axes + rep_axes)
    in_specs = (
        P(rep_axes, blk_axes, None),
        P(rep_axes, blk_axes),
        P(rep_axes, blk_axes, None),
        P(rep_axes, blk_axes),
        P(rep_axes, blk_axes, None),
        P(rep_axes, blk_axes),
        P(),
        P(),
        P(),
        P(),
    )
    out_specs = (P(rep_axes, blk_axes, None), P(), P(), P(), P())
    return jax.shard_map(
        per_device, mesh=fine, in_specs=in_specs, out_specs=out_specs, check_vma=False
    )
```

```python
import functools

import jax
import jax.numpy as jnp
import numpy as np
from jax import lax
from jax.experimental import pallas as pl
from jax.experimental.pallas import tpu as pltpu
from jax.sharding import Mesh, PartitionSpec as P

LOGIT_SCALE = 20.0
EXP_SCALE = 28.853900817779268
LEARNING_RATE = 0.5
NORM_EPS = 1e-06

BF16 = jnp.bfloat16
F32 = jnp.float32

CODE_ROWS = 16
LANES = 128


def contract_lead(left, right):
    return lax.dot_general(left, right, (((0,), (0,)), ((), ())), preferred_element_type=F32)


def contract_last(left, right):
    return lax.dot_general(left, right, (((1,), (1,)), ((), ())), preferred_element_type=F32)


def column_of(row):
    return jnp.transpose(jnp.broadcast_to(row, (LANES, row.shape[1])))


def three_pieces(values):
    high = values.astype(BF16)
    rest = values - high.astype(F32)
    middle = rest.astype(BF16)
    low = (rest - middle.astype(F32)).astype(BF16)
    return jnp.concatenate([high, middle, low], axis=1)


def add_pieces(product):
    return (product[:, 2 * LANES :] + product[:, LANES : 2 * LANES]) + product[:, :LANES]


def radius_of(outer):
    return jnp.sqrt(jnp.sum(outer * outer, axis=1, keepdims=True) + NORM_EPS)


def front_kernel(
    ids_hbm, counts_hbm, pos_hbm, table_hbm, feats_hbm, qw1_hbm, qw2_hbm, iw1_hbm, iw2_hbm,
    payload_ref, pooled_ref, tally_ref, outers_ref,
    ids_ref, counts_ref, pos_ref, table_ref, feats_ref, qw1_ref, qw2_ref, iw1_ref, iw2_ref, arrived,
):
    sources = (ids_hbm, counts_hbm, table_hbm, qw1_hbm, feats_hbm, iw1_hbm, qw2_hbm, iw2_hbm, pos_hbm)
    targets = (ids_ref, counts_ref, table_ref, qw1_ref, feats_ref, iw1_ref, qw2_ref, iw2_ref, pos_ref)
    copies = [
        pltpu.make_async_copy(source, target, arrived.at[i])
        for i, (source, target) in enumerate(zip(sources, targets))
    ]
    for copy in copies:
        copy.start()

    def tower(inputs, first, second, slot):
        pre = jnp.dot(inputs, targets[first][...], preferred_element_type=F32)
        hidden = (pre * jax.nn.sigmoid(pre)).astype(BF16)
        outer = jnp.dot(hidden, targets[second][...], preferred_element_type=F32)
        outers_ref[slot] = outer
        return (outer / radius_of(outer)).astype(BF16)

    members, q_rows = ids_ref.shape
    table_rows = table_ref.shape[0]
    copies[0].wait()
    copies[1].wait()
    counts = counts_ref[...]
    rows = lax.broadcasted_iota(jnp.int32, (table_rows, q_rows), 0)
    tally = jnp.zeros((table_rows, q_rows), F32)
    for m in range(members):
        live = jnp.where(counts > m, ids_ref[m : m + 1], -1)
        tally = tally + jnp.where(live == rows, 1.0, 0.0)
    tally = tally.astype(BF16)
    tally_ref[...] = tally
    for copy in copies[2:]:
        copy.wait()
    keys = tower(feats_ref[...], 5, 7, 1)
    product = contract_lead(tally, three_pieces(table_ref[...]))
    pooled = (add_pieces(product) / column_of(counts.astype(F32))).astype(BF16)
    pooled_ref[...] = pooled

    queries = tower(pooled, 3, 6, 0)
    pos = pos_ref[...]
    digits = jnp.concatenate([pos // LANES, pos % LANES], axis=0).astype(F32)
    spread = jnp.concatenate(
        [digits[:, i * LANES : (i + 1) * LANES] for i in range(q_rows // LANES)]
        + [jnp.zeros((CODE_ROWS - 2 * (q_rows // LANES), LANES), F32)],
        axis=0,
    ).astype(BF16)
    for copy in range(payload_ref.shape[0]):
        payload_ref[copy, :q_rows] = queries
        payload_ref[copy, q_rows : 2 * q_rows] = keys
        payload_ref[copy, 2 * q_rows :] = spread


def backward(inputs, hidden_t, slope, d_outer, second):
    d_pre = (contract_last(d_outer, second) * slope).astype(BF16)
    return contract_lead(inputs, d_pre), jnp.dot(hidden_t, d_outer, preferred_element_type=F32)


def forward(inputs, first):
    pre = jnp.dot(inputs, first, preferred_element_type=F32)
    sigma = jax.nn.sigmoid(pre)
    return jnp.transpose((pre * sigma).astype(BF16)), sigma * (1.0 + pre * (1.0 - sigma))


def prepare_kernel(
    where_ref, keep_ref, qw1_ref, qw2_ref, iw1_ref, iw2_ref,
    hidden_ref, slope_ref, first_ref, second_ref,
):
    core = where_ref[1]

    @pl.when(core == 0)
    def _():
        first_ref[...] = qw1_ref[...]
        second_ref[...] = qw2_ref[...]

    @pl.when(core != 0)
    def _():
        first_ref[...] = iw1_ref[...]
        second_ref[...] = iw2_ref[...]

    hidden_ref[...], slope_ref[...] = forward(keep_ref[keep_ref.shape[0] // 2 :], first_ref[...])


def outer_grad(d_unit, outer):
    radius = radius_of(outer)
    unit = outer / radius
    along = jnp.sum(unit * d_unit, axis=1, keepdims=True)
    return ((d_unit - unit * along) / radius).astype(BF16)


def middle_kernel(
    order, where_ref, all_ref, pos_ref, outers_ref, pooled_ref, feats_ref,
    d_query_outer_ref, keep_ref, send_ref,
    totals_ref, codes_ref, by_item_ref, by_query_ref,
):
    ranks = all_ref.shape[0]
    q_rows = outers_ref.shape[1]
    i_rows = outers_ref.shape[1]
    slot = where_ref[0]
    core = where_ref[1]
    item_start = where_ref[2] * i_rows
    norm_c = 1.0 / (q_rows * ranks)

    own_keys = all_ref[slot, q_rows : q_rows + i_rows]
    own_queries = all_ref[slot, :q_rows]

    def powers(left, right):
        return jnp.exp2(EXP_SCALE * contract_last(left, right))

    def fold(values):
        return jnp.sum(values.reshape(values.shape[0] // 8, 8, values.shape[1]), axis=0)

    own_sums = jnp.zeros((q_rows, LANES), F32)
    for s in range(ranks):
        by_item_ref[s] = powers(own_keys, all_ref[s, :q_rows])
        totals_ref[s] = fold(by_item_ref[s])
        by_query = powers(own_queries, all_ref[s, q_rows : q_rows + i_rows])
        by_query_ref[s] = by_query
        for i in range(0, i_rows, LANES):
            own_sums = own_sums + by_query[:, i : i + LANES]
        digits = all_ref[s, q_rows + i_rows :].astype(F32)
        chunks = q_rows // LANES
        code = jnp.concatenate(
            [digits[2 * i : 2 * i + 1] * LANES + digits[2 * i + 1 : 2 * i + 2] for i in range(chunks)],
            axis=1,
        )
        codes_ref[s] = jnp.broadcast_to(code.astype(jnp.int32), (8, q_rows))

    for j in range(1, ranks):
        s = lax.rem(slot + j, ranks)
        queries = all_ref[s, :q_rows]
        partial = totals_ref[s]
        for i in range(1, ranks):
            t = lax.rem(slot + i, ranks)
            partial = partial + fold(powers(all_ref[t, q_rows : q_rows + i_rows], queries))
        totals_ref[s] = jnp.broadcast_to(jnp.sum(partial, axis=0, keepdims=True), (8, q_rows))
    own_total = jnp.broadcast_to(jnp.sum(own_sums, axis=1, keepdims=True), (q_rows, LANES))
    totals_ref[slot] = jnp.transpose(own_total)[:8]

    item = item_start + lax.broadcasted_iota(jnp.int32, (i_rows, q_rows), 0)
    inverse = jnp.concatenate([norm_c / own_total] * (i_rows // LANES), axis=1)
    target = jnp.concatenate([column_of(pos_ref[...])] * (i_rows // LANES), axis=1)
    target = target - lax.broadcasted_iota(jnp.int32, (q_rows, i_rows), 1)
    d_keys = jnp.zeros((i_rows, LANES), F32)
    d_queries = jnp.zeros((q_rows, LANES), F32)
    for r in range(ranks):
        shares = by_item_ref[r] * (norm_c / totals_ref[r, :1])
        weights = (shares - jnp.where(codes_ref[r, :1] == item, norm_c, 0.0)).astype(BF16)
        d_keys = d_keys + jnp.dot(weights, all_ref[r, :q_rows], preferred_element_type=F32)
        shares = by_query_ref[r] * inverse
        weights = (shares - jnp.where(target == order[r] * i_rows, norm_c, 0.0)).astype(BF16)
        keys = all_ref[r, q_rows : q_rows + i_rows]
        d_queries = d_queries + jnp.dot(weights, keys, preferred_element_type=F32)
    d_key_outer = outer_grad(LOGIT_SCALE * d_keys, outers_ref[1])
    d_query_outer = outer_grad(LOGIT_SCALE * d_queries, outers_ref[0])
    d_query_outer_ref[...] = d_query_outer

    def split(query_ref, key_ref):
        query_ref[:q_rows] = d_query_outer
        query_ref[q_rows:] = pooled_ref[...]
        key_ref[:i_rows] = d_key_outer
        key_ref[i_rows:] = feats_ref[...]

    @pl.when(core == 0)
    def _():
        split(keep_ref, send_ref)

    @pl.when(core != 0)
    def _():
        split(send_ref, keep_ref)


def back_kernel(keep_ref, received_ref, hidden_ref, slope_ref, first_ref, second_ref, grads_ref):
    h = second_ref.shape[0]
    rows = keep_ref.shape[0] // 2
    second = second_ref[...]
    hidden_t, slope = forward(received_ref[rows:], first_ref[...])
    first_mine, second_mine = backward(keep_ref[rows:], hidden_ref[...], slope_ref[...], keep_ref[:rows], second)
    first_other, second_other = backward(received_ref[rows:], hidden_t, slope, received_ref[:rows], second)
    grads_ref[h:] = (second_mine + second_other).astype(BF16)
    first_grad = (first_mine + first_other).astype(BF16)
    for j in range(h // LANES):
        grads_ref[j * LANES : (j + 1) * LANES] = first_grad[:, j * LANES : (j + 1) * LANES]


def rows_kernel(
    tally_ref, counts_ref, pooled_ref, d_outer_ref, qw1_ref, qw2_ref, table_ref, state_ref, new_ref
):
    pre = jnp.dot(pooled_ref[...], qw1_ref[...], preferred_element_type=F32)
    sigma = jax.nn.sigmoid(pre)
    d_hidden = contract_last(d_outer_ref[...], qw2_ref[...])
    d_pre = (d_hidden * (sigma * (1.0 + pre * (1.0 - sigma)))).astype(BF16)
    d_x = contract_last(d_pre, qw1_ref[...])
    counts = column_of(counts_ref[...].astype(F32))
    pieces = three_pieces(d_x * (1.0 / counts))
    row_grads = add_pieces(jnp.dot(tally_ref[...], pieces, preferred_element_type=F32))
    mean = jnp.mean(row_grads * row_grads, axis=1, keepdims=True)
    acc = column_of(state_ref[...]) + mean
    new_ref[...] = table_ref[...] - row_grads * (LEARNING_RATE * lax.rsqrt(acc))


def finish_kernel(
    where_ref, mine_ref, other_ref, q1_ref, q2_ref, i1_ref, i2_ref, first_ref, second_ref, sent
):
    core = where_ref[1]
    h = second_ref.shape[1]

    def write(query_source, item_source):
        copies = []
        for slot, (source_ref, first_hbm, second_hbm) in enumerate(
            ((query_source, q1_ref, q2_ref), (item_source, i1_ref, i2_ref))
        ):
            second_ref[slot] = source_ref[h:].astype(F32)
            copies.append(pltpu.make_async_copy(second_ref.at[slot], second_hbm, sent.at[slot, 0]))
            copies[-1].start()
            for j in range(0, h, LANES):
                first_ref[slot, :, j : j + LANES] = source_ref[j : j + LANES].astype(F32)
            copies.append(pltpu.make_async_copy(first_ref.at[slot], first_hbm, sent.at[slot, 1]))
            copies[-1].start()
        for copy in copies:
            copy.wait()

    @pl.when(core == 0)
    def _():
        write(mine_ref, other_ref)

    @pl.when(core != 0)
    def _():
        write(other_ref, mine_ref)


VMEM = pl.BlockSpec(memory_space=pltpu.VMEM)
SMEM = pl.BlockSpec(memory_space=pltpu.SMEM)
HBM = pl.BlockSpec(memory_space=pltpu.HBM)


def call(kernel, out_shape, operands, in_specs=None, out_specs=None, scratch=(), flops=0, limit=32):
    return pl.pallas_call(
        kernel,
        out_shape=out_shape,
        in_specs=in_specs or [VMEM] * len(operands),
        out_specs=out_specs or jax.tree.map(lambda _: VMEM, out_shape),
        scratch_shapes=list(scratch),
        compiler_params=pltpu.CompilerParams(vmem_limit_bytes=limit * 2**20),
        cost_estimate=pl.CostEstimate(flops=flops, bytes_accessed=2**20, transcendentals=0),
    )(*operands)


def exchange(values, axes):
    return lax.all_to_all(values, axes, 0, 0, tiled=True)


def per_device(rows, state, bag_ids, bag_counts, item_feats, positives, q_w1, q_w2, i_w1, i_w2):
    group = ("yb", "xl", "ya")
    block = ("zp", "ya", "yb", "xh", "xl")
    strided = ("zb", "zc", "za")
    struct = jax.ShapeDtypeStruct
    ranks = lax.axis_size(group)
    spread = lax.axis_size(block)
    table = rows[0]
    feats = item_feats[0]
    q_rows, e = bag_ids.shape[1], table.shape[1]
    i_rows = feats.shape[0]
    h = q_w2.shape[0]
    blk_axes = ("ya", "yb", "xl")
    where = jnp.stack(
        [lax.axis_index(group), lax.axis_index("c"), lax.axis_index(blk_axes)]
    ).astype(jnp.int32)
    sizes = [lax.axis_size(axis) for axis in blk_axes]
    numbers = np.arange(ranks).reshape(sizes).transpose([blk_axes.index(axis) for axis in group])
    order = [int(number) for number in numbers.reshape(-1)]

    ids = bag_ids[0].T
    arguments = [ids, bag_counts, positives, table, feats, q_w1, q_w2, i_w1, i_w2]
    arguments = [pltpu.with_memory_space_constraint(a, pltpu.HBM) for a in arguments]
    payload, pooled, tally, outers = call(
        front_kernel,
        [
            struct((ranks, q_rows + i_rows + CODE_ROWS, e), BF16),
            struct((q_rows, e), BF16),
            struct((table.shape[0], q_rows), BF16),
            struct((2, q_rows, e), F32),
        ],
        arguments,
        in_specs=[HBM] * len(arguments),
        scratch=[pltpu.VMEM(a.shape, a.dtype) for a in arguments]
        + [pltpu.SemaphoreType.DMA((len(arguments),))],
    )
    payload, where = lax.optimization_barrier((payload, where))
    everyone = exchange(payload, group)
    d_query_outer, keep, send = call(
        functools.partial(middle_kernel, order),
        [struct((q_rows, e), BF16), struct((2 * q_rows, e), BF16), struct((2 * q_rows, e), BF16)],
        [where, everyone, positives, outers, pooled, feats],
        in_specs=[SMEM] + [VMEM] * 5,
        scratch=[
            pltpu.VMEM((ranks, 8, q_rows), F32),
            pltpu.VMEM((ranks, 8, q_rows), jnp.int32),
            pltpu.VMEM((ranks, i_rows, q_rows), F32),
            pltpu.VMEM((ranks, q_rows, i_rows), F32),
        ],
    )
    swap = [(0, 1), (1, 0)]
    received = lax.ppermute(send, "c", swap)
    prepared = call(
        prepare_kernel,
        [struct((h, q_rows), BF16), struct((q_rows, h), F32), struct((e, h), BF16), struct((h, e), BF16)],
        [where, keep, q_w1, q_w2, i_w1, i_w2],
        in_specs=[SMEM] + [VMEM] * 5,
        flops=2**28,
    )
    grads = call(back_kernel, struct((2 * h, e), BF16), [keep, received, *prepared])
    new_rows = call(
        rows_kernel,
        struct(table.shape, F32),
        [tally, bag_counts, pooled, d_query_outer, q_w1, q_w2, table, state],
        flops=2**30,
    )
    chip_sum = grads.reshape(spread, 2 * h // spread, e)
    mine = jnp.sum(exchange(chip_sum, block).astype(F32), axis=0).astype(BF16)
    copies = jnp.broadcast_to(mine, (lax.axis_size(strided),) + mine.shape)
    mine = jnp.sum(exchange(copies, strided).astype(F32), axis=0).astype(BF16)
    copies = jnp.broadcast_to(mine, (spread,) + mine.shape)
    tower = exchange(copies, block).reshape(2 * h, e)
    other = lax.ppermute(tower, "c", swap)
    sums = call(
        finish_kernel,
        [struct((e, h), F32), struct((h, e), F32), struct((e, h), F32), struct((h, e), F32)],
        [where, tower, other],
        in_specs=[SMEM, VMEM, VMEM],
        out_specs=[HBM] * 4,
        scratch=[
            pltpu.VMEM((2, e, h), F32),
            pltpu.VMEM((2, h, e), F32),
            pltpu.SemaphoreType.DMA((2, 2)),
        ],
    )
    return (new_rows[None], *sums)


def solution(mesh):
    blk_axes = ("ya", "yb", "xl")
    rep_axes = ("za", "zb", "zc", "zp", "xh", "c")
    parts = []
    for size, axes in zip(mesh.devices.shape, (blk_axes, rep_axes)):
        bits = size.bit_length() - 1
        parts += [1] * (len(axes) - bits) + [2] * bits
    fine = Mesh(mesh.devices.reshape(parts), blk_axes + rep_axes)
    in_specs = (
        P(rep_axes, blk_axes, None),
        P(rep_axes, blk_axes),
        P(rep_axes, blk_axes, None),
        P(rep_axes, blk_axes),
        P(rep_axes, blk_axes, None),
        P(rep_axes, blk_axes),
        P(),
        P(),
        P(),
        P(),
    )
    out_specs = (P(rep_axes, blk_axes, None), P(), P(), P(), P())
    return jax.shard_map(
        per_device, mesh=fine, in_specs=in_specs, out_specs=out_specs, check_vma=False
    )
```
